32 devices in a mesh: ctx: 8 (over z, y), tp: 4 (over x, core).
Axes of the slice: x: 2, y: 2, z: 4, core: 2. Of those that a mesh axis runs over, the one named last changes fastest.
Arguments:
- layer_input: bfloat16 [2048, 1024], P('ctx'), may hold values from -6 to 6
- attn_norm_gain: bfloat16 [1024], replicated, may hold values from 0.5 to 1.5
- attn_norm_bias: bfloat16 [1024], replicated, may hold values from -1.75 to 1.75
- mlp_norm_gain: bfloat16 [1024], replicated, may hold values from 0.5 to 1.5
- mlp_norm_bias: bfloat16 [1024], replicated, may hold values from -1.75 to 1.75
- qkv_weight: bfloat16 [1024, 3072], P(None, 'tp'), may hold values from -0.1875 to 0.1875
- qkv_bias: bfloat16 [3072], P('tp'), may hold values from -0.3125 to 0.3125
- dense_weight: bfloat16 [1024, 1024], P('tp'), may hold values from -1.5 to 1.5
- dense_bias: bfloat16 [1024], replicated, may hold values from -1.25 to 1.25
- expand_weight: bfloat16 [1024, 4096], P(None, 'tp'), may hold values from -0.1875 to 0.1875
- expand_bias: bfloat16 [4096], P('tp'), may hold values from -3 to 3
- shrink_weight: bfloat16 [4096, 1024], P('tp'), may hold values from -0.09375 to 0.09375
- shrink_bias: bfloat16 [1024], replicated, may hold values from -1.25 to 1.25
- positions: int32 [1, 2048], replicated, may hold values from 0 to 3071, as said below
- pair_table: int32 [1, 8], replicated, may hold values from 0 to 7, each once within a row
- cotangent: bfloat16 [2048, 1024], P('ctx'), may hold values from -6 to 6
Outputs:
- layer_output: bfloat16 [2048, 1024], P('ctx')
- input_grad: float32 [2048, 1024], P('ctx')
- attn_norm_gain_grad: float32 [1024], replicated
- attn_norm_bias_grad: float32 [1024], replicated
- mlp_norm_gain_grad: float32 [1024], replicated
- mlp_norm_bias_grad: float32 [1024], replicated
- qkv_weight_grad: float32 [1024, 3072], P(None, 'tp')
- qkv_bias_grad: float32 [3072], P('tp')
- dense_weight_grad: float32 [1024, 1024], P('tp')
- dense_bias_grad: float32 [1024], replicated
- expand_weight_grad: float32 [1024, 4096], P(None, 'tp')
- expand_bias_grad: float32 [4096], P('tp')
- shrink_weight_grad: float32 [4096, 1024], P('tp')
- shrink_bias_grad: float32 [1024], replicated
The draws below stay inside these ranges and needn't reach their ends.
Inputs may be any that keep to these rules, and one draw needn't show every extreme that they name: Each row of pair_table is a permutation of 0 to 7. Each row of positions starts at 0 and rises by 1 or 2 from one token to the next, by 2 at exactly 1024 of its steps.
All inputs are finite; a program needn't handle non-finite values.
Results may differ from the reference program's by a relative error of at most 0.012.
Values may be sent and summed in bfloat16 or wider, within the bound.
No kernel may reach another device: no remote copies, remote signals or barrier semaphores. Data moves between devices by JAX's collectives and lax.ppermute only.
A program may use at most 128 MiB of HBM per device.

```python
import jax
import jax.numpy as jnp
from jax import lax

D = 1024
HEADS = 16
HD = 64
ROT = 16
FF = 4096
BLK = 128
SEQS = 1
SEQ_LEN = 2048
TOKENS = 2048
N_CTX = 8


def draw_positions(key, part):
    key = jax.random.fold_in(key, 7)
    row_keys = jax.random.split(key, SEQS)
    shuffled = jax.vmap(lambda row_key: jax.random.permutation(row_key, SEQ_LEN - 1))(row_keys)
    strides = jnp.where(shuffled < SEQ_LEN // 2, 2, 1).astype(jnp.int32)
    strides = jnp.concatenate([jnp.zeros((SEQS, 1), jnp.int32), strides], axis=1)
    return jnp.cumsum(strides, axis=1, dtype=jnp.int32)


def shard_levels(rng, extent, pieces, least, largest):
    gain, own = 1.0, jax.random.fold_in(rng, 6)
    for dim, shards_of in pieces:
        draws = jnp.exp(jax.random.uniform(jax.random.fold_in(own, dim), (shards_of,), jnp.float32, least / len(pieces), largest / len(pieces)))
        gain = gain * jnp.repeat(draws, extent[dim] // shards_of).reshape([-1 if axis == dim else 1 for axis in range(len(extent))])
    return gain


def centred(stream_key, dims, scale, bound, cuts=(), kind=jnp.bfloat16):
    array = scale * jax.random.normal(stream_key, dims, jnp.float32)
    if cuts:
        array = array * shard_levels(stream_key, dims, cuts, -0.22, 0.18)
    return jnp.clip(array, -bound, bound).astype(kind)


def setup_inputs(seed: int = 0) -> dict:
    arg_keys = jax.random.split(jax.random.key(seed), 17)
    return {
        "layer_input": centred(arg_keys[0], (TOKENS, D), 1.0, 6.0, ((0, 8),)),
        "attn_norm_gain": jnp.clip(1.0 + 0.1 * jax.random.normal(arg_keys[1], (D,), jnp.float32), 0.5, 1.5).astype(jnp.bfloat16),
        "attn_norm_bias": centred(arg_keys[2], (D,), 0.3, 1.75),
        "mlp_norm_gain": jnp.clip(1.0 + 0.1 * jax.random.normal(arg_keys[3], (D,), jnp.float32), 0.5, 1.5).astype(jnp.bfloat16),
        "mlp_norm_bias": centred(arg_keys[4], (D,), 0.3, 1.75),
        "qkv_weight": centred(arg_keys[5], (D, 3 * D), D ** -0.5, 0.1875, ((1, 4),)),
        "qkv_bias": centred(arg_keys[6], (3 * D,), 0.05, 0.3125, ((0, 4),)),
        "dense_weight": centred(arg_keys[7], (D, D), 16 ** -0.5, 1.5, ((0, 4),)),
        "dense_bias": centred(arg_keys[8], (D,), 0.2, 1.25),
        "expand_weight": centred(arg_keys[9], (D, FF), D ** -0.5, 0.1875, ((1, 4),)),
        "expand_bias": centred(arg_keys[10], (FF,), 0.5, 3.0, ((0, 4),)),
        "shrink_weight": centred(arg_keys[11], (FF, D), FF ** -0.5, 0.09375, ((0, 4),)),
        "shrink_bias": centred(arg_keys[12], (D,), 0.2, 1.25),
        "positions": draw_positions(jax.random.fold_in(arg_keys[16], 71), 0),
        "pair_table": jax.vmap(lambda own: jax.random.permutation(own, N_CTX))(jax.random.split(arg_keys[14], SEQS)).reshape((SEQS, N_CTX)).astype(jnp.int32),
        "cotangent": centred(arg_keys[15], (TOKENS, D), 1.0, 6.0, ((0, 8),)),
    }


@jax.custom_vjp
def low(v):
    return lax.optimization_barrier(v.astype(jnp.bfloat16)).astype(jnp.float32)

@jax.custom_vjp
def low_back(v):
    return v

def low_keep(v):
    return (low(v), None)

def low_pass(kept, grad):
    return (grad,)

def back_keep(v):
    return (v, None)

def back_low(kept, grad):
    return (low(grad),)
low.defvjp(low_keep, low_pass)
low_back.defvjp(back_keep, back_low)

def matmul(left, right):
    return jnp.dot(left, right, precision=lax.Precision.HIGHEST, preferred_element_type=jnp.float32)

def layer_norm(values_in, norm_gain, norm_shift):
    average = lax.optimization_barrier(jnp.mean(values_in, axis=-1, keepdims=True))
    centered = values_in - average
    spread = lax.optimization_barrier(jnp.mean(centered * centered, axis=-1, keepdims=True))
    return centered * lax.rsqrt(spread + 1e-05) * norm_gain + norm_shift

def rotary_tables(places):
    frequency = 10000.0 ** (-jnp.arange(0, ROT, 2, dtype=jnp.float32) / ROT)
    angles = places[..., None] * frequency
    angles = jnp.concatenate([angles, angles], axis=-1)
    return (jnp.cos(angles), jnp.sin(angles))

def rotate(values_in, cosine, sine):
    half_rot = ROT // 2
    rotated_part = values_in[..., :ROT]
    turned = jnp.concatenate([-rotated_part[..., half_rot:], rotated_part[..., :half_rot]], axis=-1)
    return jnp.concatenate([rotated_part * cosine + turned * sine, values_in[..., ROT:]], axis=-1)

def layout_order(pair_table):
    offsets = jnp.arange(BLK, dtype=jnp.int32)
    first_block = pair_table[:, :, None] * BLK + offsets
    second_block = (2 * N_CTX - 1 - pair_table)[:, :, None] * BLK + offsets
    return jnp.concatenate([first_block, second_block], axis=2).reshape(SEQS, 2 * N_CTX * BLK)

def attend_single(items):
    queries, keys_in, values_in, token_order = items
    scores = jnp.dot(queries, keys_in.T, precision=lax.Precision.HIGHEST, preferred_element_type=jnp.float32)
    scores = low_back(scores * HD ** (-0.5))
    allowed = token_order[:, None] >= token_order[None, :]
    scores = jnp.where(allowed, scores, -1e+30)
    row_max = lax.optimization_barrier(jnp.max(scores, axis=-1, keepdims=True))
    weights = jnp.exp(scores - row_max)
    probs_low = low(weights / lax.optimization_barrier(jnp.sum(weights, axis=-1, keepdims=True)))
    return matmul(probs_low, values_in)

def forward(layer_input, attn_gain, attn_shift, mlp_gain, mlp_shift, qkv_weight, qkv_bias, dense_weight, dense_bias, expand_weight, expand_bias, shrink_weight, shrink_bias, cosine, sine, token_order):
    seq_len = 2 * N_CTX * BLK
    attn_normed = low(layer_norm(layer_input, attn_gain, attn_shift))
    mixed = low_back(matmul(attn_normed, qkv_weight) + qkv_bias)
    grouped = mixed.reshape(N_CTX, SEQS, 2 * BLK, HEADS, 3, HD).transpose(1, 3, 0, 2, 4, 5)
    grouped = grouped.reshape(SEQS, HEADS, seq_len, 3, HD)
    queries = low(rotate(grouped[..., 0, :], cosine, sine)).reshape(SEQS * HEADS, seq_len, HD)
    keys_all = low(rotate(grouped[..., 1, :], cosine, sine)).reshape(SEQS * HEADS, seq_len, HD)
    values_all = low(grouped[..., 2, :]).reshape(SEQS * HEADS, seq_len, HD)
    orders = jnp.repeat(token_order, HEADS, axis=0)
    result = lax.map(jax.checkpoint(attend_single), (queries, keys_all, values_all, orders))
    result = result.reshape(SEQS, HEADS, N_CTX, 2 * BLK, HD).transpose(2, 0, 3, 1, 4)
    attended = low(low_back(result.reshape(N_CTX * SEQS * 2 * BLK, HEADS * HD)))
    mlp_normed = low(layer_norm(layer_input, mlp_gain, mlp_shift))
    hidden = low_back(matmul(mlp_normed, expand_weight) + expand_bias)
    active = low(jax.nn.gelu(hidden, approximate=False))
    return layer_input + matmul(attended, dense_weight) + dense_bias + matmul(active, shrink_weight) + shrink_bias

def reference(layer_input, attn_norm_gain, attn_norm_bias, mlp_norm_gain, mlp_norm_bias, qkv_weight, qkv_bias, dense_weight, dense_bias, expand_weight, expand_bias, shrink_weight, shrink_bias, positions, pair_table, cotangent):
    token_order = layout_order(pair_table)
    places = jnp.take_along_axis(positions, token_order, axis=1).astype(jnp.float32)
    cosine, sine = rotary_tables(places)
    cosine = cosine[:, None]
    sine = sine[:, None]
    params = (layer_input.astype(jnp.float32), attn_norm_gain.astype(jnp.float32), attn_norm_bias.astype(jnp.float32), mlp_norm_gain.astype(jnp.float32), mlp_norm_bias.astype(jnp.float32), qkv_weight.astype(jnp.float32), qkv_bias.astype(jnp.float32), dense_weight.astype(jnp.float32), dense_bias.astype(jnp.float32), expand_weight.astype(jnp.float32), expand_bias.astype(jnp.float32), shrink_weight.astype(jnp.float32), shrink_bias.astype(jnp.float32))

    def run(*values_all):
        return forward(*values_all, cosine, sine, token_order)
    layer_output, pull_back = jax.vjp(run, *params)
    grads = pull_back(cotangent.astype(jnp.float32))
    return (layer_output.astype(jnp.bfloat16), grads[0], grads[1], grads[2], grads[3], grads[4], grads[5], grads[6], grads[7], grads[8], grads[9], grads[10], grads[11], grads[12])
```

```python
import functools

import jax
import jax.numpy as jnp
from jax import lax
from jax.experimental import pallas as pl
from jax.experimental.pallas import tpu as pltpu
from jax.sharding import PartitionSpec as P

HD = 64
ROT = 16
SCALE = HD ** (-0.5)
F32 = jnp.float32
BF16 = jnp.bfloat16
VMEM_BYTES = 56 * 1024 * 1024


def dot_nn(left, right):
    return lax.dot_general(left, right, (((1,), (0,)), ((), ())), preferred_element_type=F32)


def dot_nt(left, right):
    return lax.dot_general(left, right, (((1,), (1,)), ((), ())), preferred_element_type=F32)


def dot_tn(left, right):
    return lax.dot_general(left, right, (((0,), (0,)), ((), ())), preferred_element_type=F32)


def swap(array, axis, bits):
    return lax.ppermute(array, axis, [(i, i ^ bits) for i in range(lax.axis_size(axis))])


def params(**more):
    return pltpu.CompilerParams(vmem_limit_bytes=VMEM_BYTES, **more)


def spread_ctx(own):
    count = lax.axis_size("ctx")
    pieces = [own]
    for k in range(1, count):
        pieces.append(swap(own, "ctx", k) if k % 2 == 0 else swap(pieces[k - 1], "ctx", 1))
    return pieces


def gather_rows(own):
    count, shares = lax.axis_size("ctx"), lax.axis_size("tp")
    rows, width = own.shape
    part = rows // shares
    place = lax.axis_index("tp")
    share = lax.dynamic_slice_in_dim(own, place * part, part, 0)
    pieces = spread_ctx(share)[1:]
    bit = shares // 2
    held = [p[None] for p in pieces]
    while bit:
        upper = (place // bit) % 2
        if bit == 1:
            held = [jnp.stack(held)]
            axis = 2
        else:
            axis = 0
        others = [swap(h, "tp", bit) for h in held]
        merged = []
        for mine, other in zip(held, others):
            low = jnp.where(upper == 0, mine, other)
            high = jnp.where(upper == 0, other, mine)
            merged.append(jnp.stack([low, high], axis=1 if axis == 0 else 2))
        if axis == 0:
            held = [m.reshape(-1, part, width) for m in merged]
        else:
            held = merged
        bit //= 2
    return jnp.concatenate([own, held[0].reshape((count - 1) * rows, width)], axis=0)


def sum_tp(partial):
    shares = lax.axis_size("tp")
    place = lax.axis_index("tp")
    held = partial
    bit = 1
    while bit < shares:
        half = held.shape[0] // 2
        upper = (place // bit) % 2
        keep = lax.dynamic_slice_in_dim(held, upper * half, half, 0)
        give = lax.dynamic_slice_in_dim(held, (1 - upper) * half, half, 0)
        got = swap(give.astype(BF16), "tp", bit)
        held = keep + got.astype(F32)
        bit *= 2
    held = held.astype(BF16)
    while bit > 1:
        bit //= 2
        upper = (place // bit) % 2
        other = swap(held, "tp", bit)
        low = jnp.where(upper == 0, held, other)
        high = jnp.where(upper == 0, other, held)
        held = jnp.concatenate([low, high], axis=0)
    return held


def sum_small(partial, axes):
    held = partial
    for axis in axes:
        bit = 1
        while bit < lax.axis_size(axis):
            held = held + swap(held, axis, bit)
            bit *= 2
    return held


def rot_masks(shape):
    lane = lax.broadcasted_iota(jnp.int32, shape, 1) % HD
    return lane < ROT // 2, (lane >= ROT // 2) & (lane < ROT)


def project_kernel(x_ref, gains_ref, weight_ref, bias_ref, cos_ref, sin_ref, out_ref, attn_ref, mlp_ref):
    values = x_ref[...].astype(F32)
    average = jnp.mean(values, axis=-1, keepdims=True)
    centered = values - average
    spread = jnp.mean(centered * centered, axis=-1, keepdims=True)
    xhat = centered * lax.rsqrt(spread + 1e-05)
    attn_low = (xhat * gains_ref[0:1] + gains_ref[1:2]).astype(BF16)
    attn_ref[...] = attn_low
    mlp_ref[...] = (xhat * gains_ref[2:3] + gains_ref[3:4]).astype(BF16)
    mixed = dot_nn(attn_low, weight_ref[...]) + bias_ref[...]
    cosine, sine = cos_ref[...], sin_ref[...]
    lower, upper = rot_masks(sine.shape)
    back = jnp.where(lower, -sine, 0.0)
    ahead = jnp.where(upper, sine, 0.0)
    first = lax.broadcasted_iota(jnp.int32, sine.shape, 1) < HD
    for col in range(mixed.shape[1] // 128):
        tile = mixed[:, col * 128 : (col + 1) * 128]
        turn = [(2 * col + j) % 3 < 2 for j in range(2)]
        turned = (
            tile * cosine + pltpu.roll(tile, 120, 1) * back + pltpu.roll(tile, 8, 1) * ahead
        )
        if not turn[0]:
            turned = jnp.where(first, tile, turned)
        if not turn[1]:
            turned = jnp.where(first, turned, tile)
        out_ref[:, col * 128 : (col + 1) * 128] = turned.astype(BF16)


def project(x_all, gains, weight, bias, cosine, sine):
    rows, width = x_all.shape
    cols = weight.shape[1]
    block = 256
    row_block = lambda w: pl.BlockSpec((block, w), lambda i: (i, 0))
    whole = lambda a: pl.BlockSpec(a.shape, lambda i: (0, 0))
    return pl.pallas_call(
        project_kernel,
        grid=(rows // block,),
        in_specs=[row_block(width), whole(gains), whole(weight), whole(bias), row_block(128), row_block(128)],
        out_specs=[row_block(cols), row_block(width), row_block(width)],
        out_shape=[
            jax.ShapeDtypeStruct((rows, cols), BF16),
            jax.ShapeDtypeStruct((rows, width), BF16),
            jax.ShapeDtypeStruct((rows, width), BF16),
        ],
        compiler_params=params(),
        cost_estimate=pl.CostEstimate(
            flops=2 * rows * width * cols, bytes_accessed=rows * width * 6 + rows * cols * 2, transcendentals=0
        ),
        name="project",
    )(x_all, gains, weight, bias, cosine, sine)


def query_kernel(heads, qkv_ref, back_ref, own_ref, all_ref, out_ref, grad_ref, stats_ref):
    rows = back_ref.shape[0]
    allowed = own_ref[...] >= all_ref[...]
    columns = []
    for h in range(heads):
        base = h * 3 * HD
        queries = qkv_ref[0:rows, base : base + HD]
        keys = qkv_ref[:, base + HD : base + 2 * HD]
        values = qkv_ref[:, base + 2 * HD : base + 3 * HD]
        back = back_ref[:, h * HD : (h + 1) * HD]
        scores = jnp.where(allowed, dot_nt(queries, keys) * SCALE, -1e30)
        row_max = jnp.max(scores, axis=-1, keepdims=True)
        weights = jnp.exp(scores - row_max)
        total = jnp.sum(weights, axis=-1, keepdims=True)
        probs = weights * (1.0 / total)
        out_ref[:, h * HD : (h + 1) * HD] = dot_nn(probs.astype(BF16), values).astype(BF16)
        probs_grad = dot_nt(back, values)
        delta = jnp.sum(probs * probs_grad, axis=-1, keepdims=True)
        score_grad = (probs * (probs_grad - delta)).astype(BF16)
        grad_ref[:, h * HD : (h + 1) * HD] = dot_nn(score_grad, keys) * SCALE
        columns += [row_max + jnp.log(total), delta]
    lane = lax.broadcasted_iota(jnp.int32, (rows, 128), 1)
    table = jnp.zeros((rows, 128), F32)
    for j, column in enumerate(columns):
        table = jnp.where(lane == j, column, table)
    stats_ref[...] = table.T[: stats_ref.shape[0]]


def attend_queries(qkv, back, own_order, all_order, heads):
    rows = back.shape[0]
    keys = qkv.shape[0]
    return pl.pallas_call(
        functools.partial(query_kernel, heads),
        out_shape=[
            jax.ShapeDtypeStruct((rows, heads * HD), BF16),
            jax.ShapeDtypeStruct((rows, heads * HD), F32),
            jax.ShapeDtypeStruct((max(8, 2 * heads), rows), F32),
        ],
        compiler_params=params(),
        cost_estimate=pl.CostEstimate(
            flops=32 * heads * rows * keys * HD, bytes_accessed=qkv.size * 2, transcendentals=heads * rows * keys
        ),
        name="attend_queries",
    )(qkv, back, own_order, all_order)


def unturn(grad, cosine, sine):
    half = ROT // 2
    rotated = grad[:, :ROT]
    turned = rotated * sine[:, :ROT]
    first = rotated[:, :half] * cosine[:, :half] + turned[:, half:]
    second = rotated[:, half:] * cosine[:, half:ROT] - turned[:, :half]
    return jnp.concatenate([first, second, grad[:, ROT:]], axis=1)


def key_kernel(heads, qkv_ref, back_ref, stats_ref, own_ref, all_ref, query_grad_ref, cos_ref, sin_ref, out_ref):
    rows = query_grad_ref.shape[0]
    allowed = all_ref[...] >= own_ref[...]
    cosine, sine = cos_ref[...], sin_ref[...]
    for h in range(heads):
        base = h * 3 * HD
        queries = qkv_ref[:, base : base + HD]
        keys = qkv_ref[0:rows, base + HD : base + 2 * HD]
        values = qkv_ref[0:rows, base + 2 * HD : base + 3 * HD]
        back = back_ref[:, h * HD : (h + 1) * HD]
        lse = stats_ref[2 * h : 2 * h + 1, :]
        delta = stats_ref[2 * h + 1 : 2 * h + 2, :]
        scores = jnp.where(allowed, dot_nt(keys, queries) * SCALE - lse, -1e30)
        probs = jnp.exp(scores)
        value_grad = dot_nn(probs.astype(BF16), back)
        probs_grad = dot_nt(values, back)
        score_grad = (probs * (probs_grad - delta)).astype(BF16)
        key_grad = dot_nn(score_grad, queries) * SCALE
        query_grad = query_grad_ref[:, h * HD : (h + 1) * HD]
        out_ref[:, base : base + HD] = unturn(query_grad, cosine, sine).astype(BF16)
        out_ref[:, base + HD : base + 2 * HD] = unturn(key_grad, cosine, sine).astype(BF16)
        out_ref[:, base + 2 * HD : base + 3 * HD] = value_grad.astype(BF16)


def attend_keys(qkv, back, stats, own_order, all_order, query_grad, cosine, sine, heads):
    rows = query_grad.shape[0]
    total = qkv.shape[0]
    return pl.pallas_call(
        functools.partial(key_kernel, heads),
        out_shape=jax.ShapeDtypeStruct((rows, heads * 3 * HD), BF16),
        compiler_params=params(),
        cost_estimate=pl.CostEstimate(
            flops=32 * heads * rows * total * HD, bytes_accessed=qkv.size * 2, transcendentals=heads * rows * total
        ),
        name="attend_keys",
    )(qkv, back, stats, own_order, all_order, query_grad, cosine, sine)


def gelu_parts(hidden):
    size = jnp.abs(hidden) * (0.5 ** 0.5)
    t = 1.0 / (1.0 + 0.3275911 * size)
    bell = jnp.exp(-(size * size))
    series = 0.5 * 1.061405429
    for coefficient in (-1.453152027, 1.421413741, -0.284496736, 0.254829592):
        series = series * t + 0.5 * coefficient
    tail = series * t * bell
    phi = jnp.where(hidden >= 0, 1.0 - tail, tail)
    return hidden * phi, phi + hidden * bell * 0.3989422804014327


def gelu_kernel(mlp_ref, cot_ref, expand_ref, bias_ref, shrink_ref, active_ref, grad_ref):
    hidden = dot_nn(mlp_ref[...], expand_ref[...]) + bias_ref[...]
    active, slope = gelu_parts(hidden)
    active_ref[...] = active.astype(BF16)
    grad_ref[...] = (dot_nt(cot_ref[...], shrink_ref[...]) * slope).astype(BF16)


def gelu_branch(mlp_low, cotangent, expand, bias, shrink):
    rows, width = mlp_low.shape
    units = expand.shape[1]
    block = 256
    row_block = lambda w: pl.BlockSpec((block, w), lambda i: (i, 0))
    whole = lambda a: pl.BlockSpec(a.shape, lambda i: (0, 0))
    return pl.pallas_call(
        gelu_kernel,
        grid=(rows // block,),
        in_specs=[row_block(width), row_block(width), whole(expand), whole(bias), whole(shrink)],
        out_specs=[row_block(units), row_block(units)],
        out_shape=[jax.ShapeDtypeStruct((rows, units), BF16)] * 2,
        compiler_params=params(),
        cost_estimate=pl.CostEstimate(
            flops=4 * rows * width * units, bytes_accessed=rows * (width + units) * 4, transcendentals=rows * units
        ),
        name="gelu_branch",
    )(mlp_low, cotangent, expand, bias, shrink)


def norm_pull(back, xhat, scale, gain):
    weighted = back * gain
    mean = jnp.mean(weighted, axis=-1, keepdims=True)
    along = jnp.mean(weighted * xhat, axis=-1, keepdims=True)
    return (weighted - mean - xhat * along) * scale, jnp.sum(back * xhat, axis=0), jnp.sum(back, axis=0)


def on_device(
    layer_input,
    attn_norm_gain,
    attn_norm_bias,
    mlp_norm_gain,
    mlp_norm_bias,
    qkv_weight,
    qkv_bias,
    dense_weight,
    dense_bias,
    expand_weight,
    expand_bias,
    shrink_weight,
    shrink_bias,
    positions,
    pair_table,
    cotangent,
):
    count = lax.axis_size("ctx")
    me = lax.axis_index("ctx")
    rows = layer_input.shape[0]
    block_len = rows // 2
    heads = dense_weight.shape[0] // HD
    width = layer_input.shape[1]

    x_all = gather_rows(layer_input)
    cot_all = gather_rows(cotangent)

    pairs = pair_table[0][me ^ jnp.arange(count, dtype=jnp.int32)]
    blocks = jnp.stack([pairs, 2 * count - 1 - pairs], axis=1).reshape(-1)
    offsets = jnp.arange(block_len, dtype=jnp.int32)
    order = (blocks[:, None] * block_len + offsets).reshape(-1)
    places = positions.reshape(2 * count, block_len)[blocks].reshape(-1).astype(F32)
    lane = jnp.arange(128, dtype=jnp.int32) % HD
    frequency = jnp.where(
        lane < ROT, 10000.0 ** (-2.0 * (lane % (ROT // 2)).astype(F32) / ROT), 0.0
    )
    angles = places[:, None] * frequency[None, :]
    cosine, sine = jnp.cos(angles), jnp.sin(angles)

    gains = jnp.stack([attn_norm_gain, attn_norm_bias, mlp_norm_gain, mlp_norm_bias]).astype(F32)
    cols = qkv_weight.shape[1]
    spare = -cols % 128
    weight_wide = jnp.pad(qkv_weight, ((0, 0), (0, spare)))
    bias_wide = jnp.pad(qkv_bias, (0, spare)).astype(F32)[None]
    qkv, attn_low, mlp_low = project(x_all, gains, weight_wide, bias_wide, cosine, sine)

    back_own = dot_nt(cotangent, dense_weight).astype(BF16)
    attended, query_grad, stats = attend_queries(qkv, back_own, order[:rows, None], order[None, :], heads)
    held = stats
    bit = 1
    while bit < count:
        held = jnp.concatenate([held, swap(held, "ctx", bit)], axis=1)
        bit *= 2
    stats_all = held
    attended_all = jnp.concatenate(spread_ctx(attended), axis=0)
    back_all = dot_nt(cot_all, dense_weight).astype(BF16)
    qkv_grad = attend_keys(
        qkv, back_all, stats_all, order[:rows, None], order[None, :], query_grad, cosine[:rows], sine[:rows], heads
    )
    qkv_grad_all = jnp.concatenate(spread_ctx(qkv_grad), axis=0)

    active, hidden_grad = gelu_branch(
        mlp_low, cot_all, expand_weight, expand_bias.astype(F32)[None], shrink_weight
    )
    shrink_grad = dot_tn(active, cot_all)
    expand_grad = dot_tn(mlp_low, hidden_grad)
    expand_bias_grad = jnp.sum(hidden_grad.astype(F32), axis=0)
    bias_grad = jnp.sum(cot_all.astype(F32), axis=0)

    input_wide = layer_input.astype(F32)
    partial = dot_nn(attended, dense_weight) + dot_nn(active[:rows], shrink_weight)
    bias_total = dense_bias.astype(F32) + shrink_bias.astype(F32)
    layer_output = (input_wide + sum_tp(partial).astype(F32) + bias_total).astype(BF16)

    average = jnp.mean(input_wide, axis=-1, keepdims=True)
    centered = input_wide - average
    scale = lax.rsqrt(jnp.mean(centered * centered, axis=-1, keepdims=True) + 1e-05)
    xhat = centered * scale
    attn_back = dot_nt(qkv_grad, qkv_weight)
    mlp_back = dot_nt(hidden_grad[:rows], expand_weight)
    attn_part, attn_gain_grad, attn_bias_grad = norm_pull(attn_back, xhat, scale, gains[0:1])
    mlp_part, mlp_gain_grad, mlp_bias_grad = norm_pull(mlp_back, xhat, scale, gains[2:3])
    input_grad = cotangent.astype(F32) + sum_tp(attn_part + mlp_part).astype(F32)
    norm_grads = sum_small(
        jnp.stack([attn_gain_grad, attn_bias_grad, mlp_gain_grad, mlp_bias_grad]), ("tp", "ctx")
    )

    qkv_weight_grad = dot_tn(attn_low, qkv_grad_all)
    qkv_bias_grad = jnp.sum(qkv_grad_all.astype(F32), axis=0)
    dense_grad = dot_tn(attended_all, cot_all)
    return (
        layer_output,
        input_grad,
        norm_grads[0],
        norm_grads[1],
        norm_grads[2],
        norm_grads[3],
        qkv_weight_grad,
        qkv_bias_grad,
        dense_grad,
        bias_grad,
        expand_grad,
        expand_bias_grad,
        shrink_grad,
        bias_grad,
    )


def solution(mesh):
    placed = (
        P("ctx", None),
        P(),
        P(),
        P(),
        P(),
        P(None, "tp"),
        P("tp"),
        P("tp", None),
        P(),
        P(None, "tp"),
        P("tp"),
        P("tp", None),
        P(),
        P(),
        P(),
        P("ctx", None),
    )
    return jax.shard_map(
        on_device,
        mesh=mesh,
        in_specs=placed,
        out_specs=(
            P("ctx", None),
            P("ctx", None),
            P(),
            P(),
            P(),
            P(),
            P(None, "tp"),
            P("tp"),
            P("tp", None),
            P(),
            P(None, "tp"),
            P("tp"),
            P("tp", None),
            P(),
        ),
        check_vma=False,
    )
```

```python
import functools

import jax
import jax.numpy as jnp
from jax import lax
from jax.experimental import pallas as pl
from jax.experimental.pallas import tpu as pltpu
from jax.sharding import PartitionSpec as P

HD = 64
ROT = 16
SCALE = HD ** (-0.5)
F32 = jnp.float32
BF16 = jnp.bfloat16
VMEM_BYTES = 56 * 1024 * 1024


def dot_nn(left, right):
    return lax.dot_general(left, right, (((1,), (0,)), ((), ())), preferred_element_type=F32)


def dot_nt(left, right):
    return lax.dot_general(left, right, (((1,), (1,)), ((), ())), preferred_element_type=F32)


def dot_tn(left, right):
    return lax.dot_general(left, right, (((0,), (0,)), ((), ())), preferred_element_type=F32)


def swap(array, axis, bits):
    return lax.ppermute(array, axis, [(i, i ^ bits) for i in range(lax.axis_size(axis))])


def params(**more):
    return pltpu.CompilerParams(vmem_limit_bytes=VMEM_BYTES, **more)


def spread_ctx(own):
    count = lax.axis_size("ctx")
    pieces = [own]
    for k in range(1, count):
        pieces.append(swap(own, "ctx", k) if k % 2 == 0 else swap(pieces[k - 1], "ctx", 1))
    return pieces


def own_share(own):
    part = own.shape[0] // lax.axis_size("tp")
    return lax.dynamic_slice_in_dim(own, lax.axis_index("tp") * part, part, 0)


def gather_pieces(own):
    pieces = []
    for share in spread_ctx(own_share(own))[1:]:
        bit = lax.axis_size("tp") // 2
        shares = {0: share}
        while bit:
            for j in list(shares):
                shares[j ^ bit] = swap(shares[j], "tp", bit)
            bit //= 2
        pieces.append([shares[j] for j in range(len(shares))])
    return pieces


def sum_tp(partial):
    shares = lax.axis_size("tp")
    place = lax.axis_index("tp")
    held = partial
    bit = 1
    while bit < shares:
        half = held.shape[0] // 2
        upper = (place // bit) % 2
        keep = lax.dynamic_slice_in_dim(held, upper * half, half, 0)
        give = lax.dynamic_slice_in_dim(held, (1 - upper) * half, half, 0)
        got = swap(give.astype(BF16), "tp", bit)
        held = keep + got.astype(F32)
        bit *= 2
    held = held.astype(BF16)
    while bit > 1:
        bit //= 2
        upper = (place // bit) % 2
        other = swap(held, "tp", bit)
        low = jnp.where(upper == 0, held, other)
        high = jnp.where(upper == 0, other, held)
        held = jnp.concatenate([low, high], axis=0)
    return held


def sum_small(partial, axes):
    held = partial
    for axis in axes:
        bit = 1
        while bit < lax.axis_size(axis):
            held = held + swap(held, axis, bit)
            bit *= 2
    return held


def rot_masks(shape):
    lane = lax.broadcasted_iota(jnp.int32, shape, 1) % HD
    return lane < ROT // 2, (lane >= ROT // 2) & (lane < ROT)


def project_kernel(count, shares, place_ref, own_ref, *refs):
    parts = refs[: (count - 1) * shares]
    gains_ref, weight_ref, bias_ref, cos_ref, sin_ref, out_ref, attn_ref, mlp_ref = refs[(count - 1) * shares :]
    step = pl.program_id(0)

    def normalize(part_ref, rows):
        values = part_ref[...].astype(F32)
        average = jnp.mean(values, axis=-1, keepdims=True)
        centered = values - average
        spread = jnp.mean(centered * centered, axis=-1, keepdims=True)
        xhat = centered * lax.rsqrt(spread + 1e-05)
        attn_ref[rows, :] = (xhat * gains_ref[0:1] + gains_ref[1:2]).astype(BF16)
        mlp_ref[rows, :] = (xhat * gains_ref[2:3] + gains_ref[3:4]).astype(BF16)

    @pl.when(step == 0)
    def _():
        normalize(own_ref, slice(None))

    for k in range(1, count):

        @pl.when(step == k)
        def _():
            for j in range(shares):
                part_ref = parts[(k - 1) * shares + j]
                size = part_ref.shape[0]
                normalize(part_ref, pl.ds(pl.multiple_of((place_ref[1] ^ j) * size, size), size))

    mixed = dot_nn(attn_ref[...], weight_ref[...]) + bias_ref[...]
    cosine, sine = cos_ref[...], sin_ref[...]
    lower, upper = rot_masks(sine.shape)
    back = jnp.where(lower, -sine, 0.0)
    ahead = jnp.where(upper, sine, 0.0)
    first = lax.broadcasted_iota(jnp.int32, sine.shape, 1) < HD
    for col in range(mixed.shape[1] // 128):
        tile = mixed[:, col * 128 : (col + 1) * 128]
        turn = [(2 * col + j) % 3 < 2 for j in range(2)]
        turned = (
            tile * cosine + pltpu.roll(tile, 120, 1) * back + pltpu.roll(tile, 8, 1) * ahead
        )
        if not turn[0]:
            turned = jnp.where(first, tile, turned)
        if not turn[1]:
            turned = jnp.where(first, turned, tile)
        out_ref[:, col * 128 : (col + 1) * 128] = turned.astype(BF16)


def project(me, place, own, pieces, gains, weight, bias, cosine, sine):
    total = cosine.shape[0]
    rows, width = own.shape
    cols = weight.shape[1]
    count, shares = len(pieces) + 1, len(pieces[0])
    parts = [part for piece in pieces for part in piece]
    row_block = lambda w: pl.BlockSpec((rows, w), lambda i, place_ref: (place_ref[0] ^ i, 0))
    whole = lambda a: pl.BlockSpec(a.shape, lambda i, place_ref: (0, 0))
    return pl.pallas_call(
        functools.partial(project_kernel, count, shares),
        grid_spec=pltpu.PrefetchScalarGridSpec(
            num_scalar_prefetch=1,
            grid=(count,),
            in_specs=[whole(own)]
            + [whole(p) for p in parts]
            + [whole(gains), whole(weight), whole(bias), row_block(128), row_block(128)],
            out_specs=[row_block(cols), row_block(width), row_block(width)],
        ),
        out_shape=[
            jax.ShapeDtypeStruct((total, cols), BF16),
            jax.ShapeDtypeStruct((total, width), BF16),
            jax.ShapeDtypeStruct((total, width), BF16),
        ],
        compiler_params=params(),
        cost_estimate=pl.CostEstimate(
            flops=2 * total * width * cols, bytes_accessed=total * width * 6 + total * cols * 2, transcendentals=0
        ),
        name="project",
    )(jnp.stack([me, place]), own, *parts, gains, weight, bias, cosine, sine)


def unturn(grad, cosine, sine):
    half = ROT // 2
    rotated = grad[:, :ROT]
    turned = rotated * sine[:, :ROT]
    first = rotated[:, :half] * cosine[:, :half] + turned[:, half:]
    second = rotated[:, half:] * cosine[:, half:ROT] - turned[:, :half]
    return jnp.concatenate([first, second, grad[:, ROT:]], axis=1)


def query_kernel(heads, me_ref, qkv_ref, back_ref, own_ref, all_ref, cos_ref, sin_ref, out_ref, stats_ref):
    rows = back_ref.shape[0]
    mine = pl.ds(pl.multiple_of(me_ref[0] * rows, rows), rows)
    allowed = own_ref[...] >= all_ref[...]
    cosine, sine = cos_ref[mine, :], sin_ref[mine, :]
    columns = []
    for h in range(heads):
        base = h * 3 * HD
        queries = qkv_ref[mine, base : base + HD]
        keys = qkv_ref[:, base + HD : base + 2 * HD]
        values = qkv_ref[:, base + 2 * HD : base + 3 * HD]
        back = back_ref[:, h * HD : (h + 1) * HD]
        scores = jnp.where(allowed, dot_nt(queries, keys) * SCALE, -1e30)
        row_max = jnp.max(scores, axis=-1, keepdims=True)
        weights = jnp.exp(scores - row_max)
        total = jnp.sum(weights, axis=-1, keepdims=True)
        probs = weights * (1.0 / total)
        out_ref[:, h * HD : (h + 1) * HD] = dot_nn(probs.astype(BF16), values).astype(BF16)
        probs_grad = dot_nt(back, values)
        delta = jnp.sum(probs * probs_grad, axis=-1, keepdims=True)
        score_grad = (probs * (probs_grad - delta)).astype(BF16)
        query_grad = unturn(dot_nn(score_grad, keys) * SCALE, cosine, sine)
        out_ref[:, (heads + h) * HD : (heads + h + 1) * HD] = query_grad.astype(BF16)
        columns += [row_max + jnp.log(total), delta]
    lane = lax.broadcasted_iota(jnp.int32, (rows, 128), 1)
    table = jnp.zeros((rows, 128), F32)
    for j, column in enumerate(columns):
        table = jnp.where(lane == j, column, table)
    stats_ref[...] = table.T[: stats_ref.shape[0]]


VMEM_SPEC = pl.BlockSpec(memory_space=pltpu.VMEM)
SMEM_SPEC = pl.BlockSpec(memory_space=pltpu.SMEM)


def attend_queries(me, qkv, back, own_order, all_order, cosine, sine, heads):
    rows = back.shape[0]
    keys = qkv.shape[0]
    return pl.pallas_call(
        functools.partial(query_kernel, heads),
        in_specs=[SMEM_SPEC] + [VMEM_SPEC] * 6,
        out_shape=[
            jax.ShapeDtypeStruct((rows, 2 * heads * HD), BF16),
            jax.ShapeDtypeStruct((max(8, 2 * heads), rows), F32),
        ],
        compiler_params=params(),
        cost_estimate=pl.CostEstimate(
            flops=32 * heads * rows * keys * HD, bytes_accessed=qkv.size * 2, transcendentals=heads * rows * keys
        ),
        name="attend_queries",
    )(me, qkv, back, own_order, all_order, cosine, sine)


def key_kernel(heads, me_ref, qkv_ref, back_ref, stats_ref, own_ref, all_ref, cos_ref, sin_ref, adq_ref, out_ref):
    rows = out_ref.shape[0]
    count = qkv_ref.shape[0] // rows
    me = me_ref[0]
    mine = pl.ds(pl.multiple_of(me * rows, rows), rows)
    own_order = own_ref[...]
    cosine, sine = cos_ref[mine, :], sin_ref[mine, :]
    for h in range(heads):
        base = h * 3 * HD
        keys = qkv_ref[mine, base + HD : base + 2 * HD]
        values = qkv_ref[mine, base + 2 * HD : base + 3 * HD]
        key_grad = jnp.zeros((rows, HD), F32)
        value_grad = jnp.zeros((rows, HD), F32)
        for j in range(count):
            span = slice(j * rows, (j + 1) * rows)
            queries = qkv_ref[span, base : base + HD]
            back = back_ref[span, h * HD : (h + 1) * HD]
            stats = stats_ref[me ^ j]
            lse = stats[2 * h : 2 * h + 1, :]
            delta = stats[2 * h + 1 : 2 * h + 2, :]
            allowed = all_ref[:, span] >= own_order
            probs = jnp.exp(jnp.where(allowed, dot_nt(keys, queries) * SCALE - lse, -1e30))
            value_grad += dot_nn(probs.astype(BF16), back)
            probs_grad = dot_nt(values, back)
            score_grad = (probs * (probs_grad - delta)).astype(BF16)
            key_grad += dot_nn(score_grad, queries)
        out_ref[:, base : base + HD] = adq_ref[:, (heads + h) * HD : (heads + h + 1) * HD]
        out_ref[:, base + HD : base + 2 * HD] = unturn(key_grad * SCALE, cosine, sine).astype(BF16)
        out_ref[:, base + 2 * HD : base + 3 * HD] = value_grad.astype(BF16)


def attend_keys(me, qkv, back, stats, own_order, all_order, cosine, sine, adq, heads):
    rows = own_order.shape[0]
    total = qkv.shape[0]
    return pl.pallas_call(
        functools.partial(key_kernel, heads),
        in_specs=[SMEM_SPEC] + [VMEM_SPEC] * 8,
        out_shape=jax.ShapeDtypeStruct((rows, heads * 3 * HD), BF16),
        compiler_params=params(),
        cost_estimate=pl.CostEstimate(
            flops=32 * heads * rows * total * HD, bytes_accessed=qkv.size * 2, transcendentals=heads * rows * total
        ),
        name="attend_keys",
    )(me, qkv, back, stats, own_order, all_order, cosine, sine, adq)


def dense_kernel(count, me_ref, cot_ref, *refs):
    pieces = refs[:count]
    out_ref, attended_ref = refs[count:]
    rows, cols = pieces[0].shape[0], out_ref.shape[0]

    @pl.when(pl.program_id(0) == 0)
    def _():
        for k, piece in enumerate(pieces):
            at = pl.ds(pl.multiple_of((me_ref[0] ^ k) * rows, rows), rows)
            attended_ref[at, :] = piece[...]

    out_ref[...] = dot_tn(attended_ref[...], cot_ref[...])


def dense_weight_grads(me, cot_all, pieces):
    total, width = cot_all.shape
    cols = pieces[0].shape[1]
    tile = 512
    whole = lambda a: pl.BlockSpec(a.shape, lambda i: (0, 0))
    return pl.pallas_call(
        functools.partial(dense_kernel, len(pieces)),
        grid=(width // tile,),
        in_specs=[SMEM_SPEC, pl.BlockSpec((total, tile), lambda i: (0, i))] + [whole(p) for p in pieces],
        out_specs=pl.BlockSpec((cols, tile), lambda i: (0, i)),
        out_shape=jax.ShapeDtypeStruct((cols, width), F32),
        scratch_shapes=[pltpu.VMEM((total, cols), BF16)],
        compiler_params=params(),
        cost_estimate=pl.CostEstimate(
            flops=2 * total * width * cols, bytes_accessed=total * width * 2 + width * cols * 4, transcendentals=0
        ),
        name="dense_weight_grads",
    )(me, cot_all, *pieces)


def gelu_parts(hidden):
    size = jnp.abs(hidden) * (0.5 ** 0.5)
    t = 1.0 / (1.0 + 0.3275911 * size)
    bell = jnp.exp(-(size * size))
    series = 0.5 * 1.061405429
    for coefficient in (-1.453152027, 1.421413741, -0.284496736, 0.254829592):
        series = series * t + 0.5 * coefficient
    tail = series * t * bell
    phi = jnp.where(hidden >= 0, 1.0 - tail, tail)
    return hidden * phi, phi + hidden * bell * 0.3989422804014327


def gelu_kernel(carried, mlp_ref, cot_ref, expand_ref, bias_ref, shrink_ref, *refs):
    active_ref, grad_ref = refs[carried:]
    hidden = dot_nn(mlp_ref[...], expand_ref[...]) + bias_ref[...]
    active, slope = gelu_parts(hidden)
    active_ref[...] = active.astype(BF16)
    grad_ref[...] = (dot_nt(cot_ref[...], shrink_ref[...]) * slope).astype(BF16)


def gelu_branch(mlp_low, cotangent, expand, bias, shrink, start, blocks, carried=()):
    rows, width = mlp_low.shape
    units = expand.shape[1]
    block = 256
    row_block = lambda w: pl.BlockSpec((block, w), lambda i: (i + start, 0))
    whole = lambda a: pl.BlockSpec(a.shape, lambda i: (0, 0))
    return pl.pallas_call(
        functools.partial(gelu_kernel, len(carried)),
        grid=(blocks,),
        in_specs=[row_block(width), row_block(width), whole(expand), whole(bias), whole(shrink)]
        + [pl.BlockSpec(memory_space=pl.ANY)] * len(carried),
        out_specs=[row_block(units), row_block(units)],
        out_shape=[jax.ShapeDtypeStruct((rows, units), BF16)] * 2,
        input_output_aliases={5 + j: j for j in range(len(carried))},
        compiler_params=params(),
        cost_estimate=pl.CostEstimate(
            flops=4 * blocks * block * width * units,
            bytes_accessed=blocks * block * (width + units) * 4,
            transcendentals=blocks * block * units,
        ),
        name="gelu_branch",
    )(mlp_low, cotangent, expand, bias, shrink, *carried)


def norm_pull(back, xhat, scale, gain):
    weighted = back * gain
    mean = jnp.mean(weighted, axis=-1, keepdims=True)
    along = jnp.mean(weighted * xhat, axis=-1, keepdims=True)
    return (weighted - mean - xhat * along) * scale, jnp.sum(back * xhat, axis=0), jnp.sum(back, axis=0)


def on_device(
    layer_input,
    attn_norm_gain,
    attn_norm_bias,
    mlp_norm_gain,
    mlp_norm_bias,
    qkv_weight,
    qkv_bias,
    dense_weight,
    dense_bias,
    expand_weight,
    expand_bias,
    shrink_weight,
    shrink_bias,
    positions,
    pair_table,
    cotangent,
):
    count = lax.axis_size("ctx")
    me = lax.axis_index("ctx")
    rows = layer_input.shape[0]
    block_len = rows // 2
    heads = dense_weight.shape[0] // HD
    width = layer_input.shape[1]

    place = lax.axis_index("tp")
    me_table = me.reshape(1).astype(jnp.int32)
    cot_all = lax.all_gather(own_share(cotangent), ("ctx", "tp"), axis=0, tiled=True)
    pieces = gather_pieces(layer_input)

    pairs = pair_table[0]
    blocks = jnp.stack([pairs, 2 * count - 1 - pairs], axis=1).reshape(-1)
    offsets = jnp.arange(block_len, dtype=jnp.int32)
    order = (blocks[:, None] * block_len + offsets).reshape(-1)
    own_order = lax.dynamic_slice_in_dim(order, me * rows, rows, 0)[:, None]
    places = positions.reshape(2 * count, block_len)[blocks].reshape(-1).astype(F32)
    lane = jnp.arange(128, dtype=jnp.int32) % HD
    frequency = jnp.where(
        lane < ROT, 10000.0 ** (-2.0 * (lane % (ROT // 2)).astype(F32) / ROT), 0.0
    )
    angles = places[:, None] * frequency[None, :]
    cosine, sine = jnp.cos(angles), jnp.sin(angles)

    gains = jnp.stack([attn_norm_gain, attn_norm_bias, mlp_norm_gain, mlp_norm_bias]).astype(F32)
    cols = qkv_weight.shape[1]
    spare = -cols % 128
    weight_wide = jnp.pad(qkv_weight, ((0, 0), (0, spare)))
    bias_wide = jnp.pad(qkv_bias, (0, spare)).astype(F32)[None]
    qkv, attn_low, mlp_low = project(
        me, place, layer_input, pieces, gains, weight_wide, bias_wide, cosine, sine
    )

    expand_bias_wide = expand_bias.astype(F32)[None]
    back_own = dot_nt(cotangent, dense_weight).astype(BF16)
    adq, stats = attend_queries(me_table, qkv, back_own, own_order, order[None, :], cosine, sine, heads)
    stats_all = stats[None]
    bit = 1
    while bit < count:
        stats_all = jnp.concatenate([stats_all, swap(stats_all, "ctx", bit)], axis=0)
        bit *= 2
    attended = adq[:, : heads * HD]
    attended_pieces = spread_ctx(attended)
    back_all = dot_nt(cot_all, dense_weight).astype(BF16)
    qkv_grad = attend_keys(
        me_table, qkv, back_all, stats_all, own_order, order[None, :], cosine, sine, adq, heads
    )
    qkv_grad_all = lax.all_gather(qkv_grad, "ctx", axis=0, tiled=True)

    mlp_low, qkv_grad = lax.optimization_barrier((mlp_low, qkv_grad))
    active, hidden_grad = gelu_branch(
        mlp_low, cot_all, expand_weight, expand_bias_wide, shrink_weight, 0, count
    )
    active_own = lax.dynamic_slice_in_dim(active, me * rows, rows, 0)
    hidden_grad_own = lax.dynamic_slice_in_dim(hidden_grad, me * rows, rows, 0)
    shrink_grad = dot_tn(active, cot_all)
    expand_grad = dot_tn(mlp_low, hidden_grad)
    expand_bias_grad = jnp.sum(hidden_grad.astype(F32), axis=0)
    bias_grad = jnp.sum(cot_all.astype(F32), axis=0)

    input_wide = layer_input.astype(F32)
    partial = dot_nn(attended, dense_weight) + dot_nn(active_own, shrink_weight)
    bias_total = dense_bias.astype(F32) + shrink_bias.astype(F32)
    layer_output = (input_wide + sum_tp(partial).astype(F32) + bias_total).astype(BF16)

    average = jnp.mean(input_wide, axis=-1, keepdims=True)
    centered = input_wide - average
    scale = lax.rsqrt(jnp.mean(centered * centered, axis=-1, keepdims=True) + 1e-05)
    xhat = centered * scale
    attn_back = dot_nt(qkv_grad, qkv_weight)
    mlp_back = dot_nt(hidden_grad_own, expand_weight)
    attn_part, attn_gain_grad, attn_bias_grad = norm_pull(attn_back, xhat, scale, gains[0:1])
    mlp_part, mlp_gain_grad, mlp_bias_grad = norm_pull(mlp_back, xhat, scale, gains[2:3])
    input_grad = cotangent.astype(F32) + sum_tp(attn_part + mlp_part).astype(F32)
    norm_grads = sum_small(
        jnp.stack([attn_gain_grad, attn_bias_grad, mlp_gain_grad, mlp_bias_grad]), ("tp", "ctx")
    )

    qkv_weight_grad = dot_tn(attn_low, qkv_grad_all)
    qkv_bias_grad = jnp.sum(qkv_grad_all.astype(F32), axis=0)
    dense_grad = dense_weight_grads(me_table, cot_all, attended_pieces)
    return (
        layer_output,
        input_grad,
        norm_grads[0],
        norm_grads[1],
        norm_grads[2],
        norm_grads[3],
        qkv_weight_grad,
        qkv_bias_grad,
        dense_grad,
        bias_grad,
        expand_grad,
        expand_bias_grad,
        shrink_grad,
        bias_grad,
    )


def solution(mesh):
    placed = (
        P("ctx", None),
        P(),
        P(),
        P(),
        P(),
        P(None, "tp"),
        P("tp"),
        P("tp", None),
        P(),
        P(None, "tp"),
        P("tp"),
        P("tp", None),
        P(),
        P(),
        P(),
        P("ctx", None),
    )
    return jax.shard_map(
        on_device,
        mesh=mesh,
        in_specs=placed,
        out_specs=(
            P("ctx", None),
            P("ctx", None),
            P(),
            P(),
            P(),
            P(),
            P(None, "tp"),
            P("tp"),
            P("tp", None),
            P(),
            P(None, "tp"),
            P("tp"),
            P("tp", None),
            P(),
        ),
        check_vma=False,
    )
```

```python
import functools

import jax
import jax.numpy as jnp
from jax import lax
from jax.experimental import pallas as pl
from jax.experimental.pallas import tpu as pltpu
from jax.sharding import PartitionSpec as P

HD = 64
ROT = 16
SCALE = HD ** (-0.5)
F32 = jnp.float32
BF16 = jnp.bfloat16
MIB = 1024 * 1024


def dot_nn(left, right):
    return lax.dot_general(left, right, (((1,), (0,)), ((), ())), preferred_element_type=F32)


def dot_nt(left, right):
    return lax.dot_general(left, right, (((1,), (1,)), ((), ())), preferred_element_type=F32)


def dot_tn(left, right):
    return lax.dot_general(left, right, (((0,), (0,)), ((), ())), preferred_element_type=F32)


def swap(array, axis, bits):
    return lax.ppermute(array, axis, [(i, i ^ bits) for i in range(lax.axis_size(axis))])


def params(mib):
    return pltpu.CompilerParams(vmem_limit_bytes=mib * MIB)


VMEM_SPEC = pl.BlockSpec(memory_space=pltpu.VMEM)
SMEM_SPEC = pl.BlockSpec(memory_space=pltpu.SMEM)
ANY_SPEC = pl.BlockSpec(memory_space=pl.ANY)


def spread_ctx(own):
    count = lax.axis_size("ctx")
    pieces = [own]
    for k in range(1, count):
        pieces.append(swap(own, "ctx", k) if k % 2 == 0 else swap(pieces[k - 1], "ctx", 1))
    return pieces


def own_share(own):
    part = own.shape[0] // lax.axis_size("tp")
    return lax.dynamic_slice_in_dim(own, lax.axis_index("tp") * part, part, 0)


def gather_pieces(own, beside):
    count, shares = lax.axis_size("ctx"), lax.axis_size("tp")
    share = own_share(own)
    near = [1] + list(range(2, count, 2))
    far = list(range(3, count, 2))
    arrived = {(k, 0): swap(share, "ctx", k) for k in near}
    arrived, beside = tie(arrived, beside)
    levels = shares.bit_length() - 1

    def level(pieces, number):
        for k in pieces:
            for j in range(1, shares):
                if bin(j).count("1") == number:
                    low = j & -j
                    yield (k, j), swap(arrived[k, j ^ low], "tp", low)

    for stage in range(1, levels + 2):
        found = {}
        if stage == 1:
            found.update({(k, 0): swap(arrived[k - 1, 0], "ctx", 1) for k in far})
        found.update(level(near, stage))
        found.update(level(far, stage - 1))
        arrived.update(found)
    return [[arrived[k, j] for j in range(shares)] for k in range(1, count)], beside


def tie(*items):
    return lax.optimization_barrier(items if len(items) > 1 else items[0])


def after(array, other):
    return tie(array, other)[0]


def sum_tp(partial):
    shares = lax.axis_size("tp")
    place = lax.axis_index("tp")
    held = partial
    bit = 1
    while bit < shares:
        half = held.shape[1] // 2
        upper = (place // bit) % 2
        keep = lax.dynamic_slice_in_dim(held, upper * half, half, 1)
        give = lax.dynamic_slice_in_dim(held, (1 - upper) * half, half, 1)
        got = yield swap(give.astype(BF16), "tp", bit)
        held = keep + got.astype(F32)
        bit *= 2
    held = held.astype(BF16)
    while bit > 1:
        bit //= 2
        upper = (place // bit) % 2
        other = yield swap(held, "tp", bit)
        low = jnp.where(upper == 0, held, other)
        high = jnp.where(upper == 0, other, held)
        held = jnp.concatenate([low, high], axis=1)
    return held


def sum_small(partial, axes):
    held = partial
    for axis in axes:
        bit = 1
        while bit < lax.axis_size(axis):
            got = yield swap(held, axis, bit)
            held = held + got
            bit *= 2
    return held


def overlap(chains, steps):
    flying = {i: next(chain) for i, chain in enumerate(chains)}
    ends, results = {}, []

    def advance(arrived):
        for i, got in arrived.items():
            try:
                flying[i] = chains[i].send(got)
            except StopIteration as stop:
                ends[i] = stop.value
                del flying[i]

    operands = steps[0][1]
    for number, (run, _) in enumerate(steps):
        result = run(*operands)
        following = steps[number + 1][1] if number + 1 < len(steps) else ()
        arrived, result, operands = tie(dict(flying), result, tuple(following))
        results.append(result)
        advance(arrived)
    while flying:
        advance(dict(flying))
    return [ends[i] for i in range(len(chains))], results


def column_sums(array):
    return dot_nn(jnp.ones((8, array.shape[0]), BF16), array)[0]


def rot_masks(shape):
    lane = lax.broadcasted_iota(jnp.int32, shape, 1) % HD
    return lane < ROT // 2, (lane >= ROT // 2) & (lane < ROT)


def rot_tables(compact):
    shape = (4 * (ROT // 2), 256)
    row, column = lax.broadcasted_iota(jnp.int32, shape, 0), lax.broadcasted_iota(jnp.int32, shape, 1)
    lane = column % HD
    hit = (lane < ROT) & (lane % (ROT // 2) == row % (ROT // 2)) & (column // 128 == row // ROT)
    both = dot_tn(compact, jnp.where(hit, 1.0, 0.0).astype(BF16))
    still = lax.broadcasted_iota(jnp.int32, (compact.shape[1], 128), 1) % HD >= ROT
    return jnp.where(still, 1.0, both[:, :128]), both[:, 128:]


def split_turns(angles):
    parts = []
    for table in (jnp.cos(angles), jnp.sin(angles)):
        high = lax.reduce_precision(table, 8, 7)
        parts += [high.astype(BF16), (table - high).astype(BF16)]
    return jnp.concatenate(parts, axis=0)


def project_kernel(groups, place_ref, *refs):
    parts = [refs[sum(groups[:g]) : sum(groups[: g + 1])] for g in range(len(groups))]
    gains_ref, weight_ref, bias_ref, turn_ref, out_ref, xhat_ref, x_ref, sems = refs[sum(groups) :]
    step = pl.program_id(0)
    count, shares = len(groups), groups[-1]

    def load(g, act):
        slot = g % 2
        for j, part in enumerate(parts[g]):
            size = part.shape[0]
            at = place_ref[0] ^ j if len(parts[g]) > 1 else 0
            rows = pl.ds(pl.multiple_of(at * size, size), size)
            act(pltpu.make_async_copy(part, x_ref.at[slot, rows, :], sems.at[slot, j]))

    for g in range(count):

        @pl.when(step == g)
        def _():
            if g == 0:
                load(0, lambda copy: copy.start())
            if g + 1 < count:
                load(g + 1, lambda copy: copy.start())
            load(g, lambda copy: copy.wait())

    values = x_ref[step % 2].astype(F32)
    average = jnp.mean(values, axis=-1, keepdims=True)
    centered = values - average
    spread = jnp.mean(centered * centered, axis=-1, keepdims=True)
    xhat = centered * lax.rsqrt(spread + 1e-05)
    xhat_ref[...] = xhat.astype(BF16)
    low = (xhat * gains_ref[0:1] + gains_ref[1:2]).astype(BF16)
    mixed = dot_nn(low, weight_ref[...]) + bias_ref[...]
    cosine, sine = rot_tables(turn_ref[...])
    lower, upper = rot_masks(sine.shape)
    back = jnp.where(lower, -sine, 0.0)
    ahead = jnp.where(upper, sine, 0.0)
    first = lax.broadcasted_iota(jnp.int32, sine.shape, 1) < HD
    rows = mixed.shape[0]
    mine = pl.ds(pl.multiple_of(place_ref[1 + step] * rows, rows), rows)
    for col in range(mixed.shape[1] // 128):
        tile = mixed[:, col * 128 : (col + 1) * 128]
        turn = [(2 * col + j) % 3 < 2 for j in range(2)]
        turned = (
            tile * cosine + pltpu.roll(tile, 120, 1) * back + pltpu.roll(tile, 8, 1) * ahead
        )
        if not turn[0]:
            turned = jnp.where(first, tile, turned)
        if not turn[1]:
            turned = jnp.where(first, turned, tile)
        out_ref[mine, col * 128 : (col + 1) * 128] = turned.astype(BF16)


def project(place, owners, pieces, gains, weight, bias, turns):
    total = turns.shape[1]
    groups = tuple(len(piece) for piece in pieces)
    parts = [part for piece in pieces for part in piece]
    rows, width = sum(part.shape[0] for part in pieces[0]), parts[0].shape[1]
    cols = weight.shape[1]
    whole = lambda a: pl.BlockSpec(a.shape, lambda i, place_ref: (0, 0))
    return pl.pallas_call(
        functools.partial(project_kernel, groups),
        grid_spec=pltpu.PrefetchScalarGridSpec(
            num_scalar_prefetch=1,
            grid=(len(pieces),),
            in_specs=[ANY_SPEC] * len(parts)
            + [whole(gains), whole(weight), whole(bias)]
            + [pl.BlockSpec((turns.shape[0], rows), lambda i, place_ref: (0, place_ref[1 + i]))],
            out_specs=[VMEM_SPEC, pl.BlockSpec((rows, width), lambda i, place_ref: (place_ref[1 + i], 0))],
            scratch_shapes=[
                pltpu.VMEM((2, rows, width), BF16),
                pltpu.SemaphoreType.DMA((2, max(groups))),
            ],
        ),
        out_shape=[jax.ShapeDtypeStruct((total, cols), BF16), jax.ShapeDtypeStruct((total, width), BF16)],
        compiler_params=params(56),
        cost_estimate=pl.CostEstimate(
            flops=2 * total * width * cols, bytes_accessed=total * width * 4 + total * cols * 2, transcendentals=0
        ),
        name="project",
    )(jnp.stack([place] + owners), *parts, gains, weight, bias, turns)


def unturn(grad, cosine, sine):
    half = ROT // 2
    rotated = grad[:, :ROT]
    turned = rotated * sine[:, :ROT]
    first = rotated[:, :half] * cosine[:, :half] + turned[:, half:]
    second = rotated[:, half:] * cosine[:, half:ROT] - turned[:, :half]
    return jnp.concatenate([first, second, grad[:, ROT:]], axis=1)


def query_kernel(heads, me_ref, qkv_ref, back_ref, own_ref, all_ref, turn_ref, out_ref, stats_ref):
    rows = back_ref.shape[0]
    mine = pl.ds(pl.multiple_of(me_ref[0] * rows, rows), rows)
    allowed = own_ref[...] >= all_ref[...]
    cosine, sine = rot_tables(turn_ref[...])
    columns = []
    for h in range(heads):
        base = h * 3 * HD
        queries = qkv_ref[mine, base : base + HD]
        keys = qkv_ref[:, base + HD : base + 2 * HD]
        values = qkv_ref[:, base + 2 * HD : base + 3 * HD]
        back = back_ref[:, h * HD : (h + 1) * HD]
        scores = jnp.where(allowed, dot_nt(queries, keys) * SCALE, -1e30)
        row_max = jnp.max(scores, axis=-1, keepdims=True)
        weights = jnp.exp(scores - row_max)
        total = jnp.sum(weights, axis=-1, keepdims=True)
        probs = weights * (1.0 / total)
        out_ref[:, h * HD : (h + 1) * HD] = dot_nn(probs.astype(BF16), values).astype(BF16)
        probs_grad = dot_nt(back, values)
        delta = jnp.sum(probs * probs_grad, axis=-1, keepdims=True)
        score_grad = (probs * (probs_grad - delta)).astype(BF16)
        query_grad = unturn(dot_nn(score_grad, keys) * SCALE, cosine, sine)
        out_ref[:, (heads + h) * HD : (heads + h + 1) * HD] = query_grad.astype(BF16)
        columns += [row_max + jnp.log(total), delta]
    lane = lax.broadcasted_iota(jnp.int32, (rows, 128), 1)
    table = jnp.zeros((rows, 128), F32)
    for j, column in enumerate(columns):
        table = jnp.where(lane == j, column, table)
    stats_ref[...] = table.T[: stats_ref.shape[0]]


def attend_queries(me, qkv, back, own_order, all_order, turns, heads):
    rows = back.shape[0]
    keys = qkv.shape[0]
    return pl.pallas_call(
        functools.partial(query_kernel, heads),
        in_specs=[SMEM_SPEC] + [VMEM_SPEC] * 5,
        out_shape=[
            jax.ShapeDtypeStruct((rows, 2 * heads * HD), BF16),
            jax.ShapeDtypeStruct((max(8, 2 * heads), rows), F32),
        ],
        compiler_params=params(56),
        cost_estimate=pl.CostEstimate(
            flops=32 * heads * rows * keys * HD, bytes_accessed=qkv.size * 2, transcendentals=heads * rows * keys
        ),
        name="attend_queries",
    )(me, qkv, back, own_order, all_order, turns)


def key_kernel(heads, me_ref, qkv_ref, back_ref, stats_ref, own_ref, all_ref, turn_ref, adq_ref, out_ref):
    rows = out_ref.shape[0]
    count = qkv_ref.shape[0] // rows
    me = me_ref[0]
    mine = pl.ds(pl.multiple_of(me * rows, rows), rows)
    own_order = own_ref[...]
    cosine, sine = rot_tables(turn_ref[...])
    for h in range(heads):
        base = h * 3 * HD
        keys = qkv_ref[mine, base + HD : base + 2 * HD]
        values = qkv_ref[mine, base + 2 * HD : base + 3 * HD]
        key_grad = jnp.zeros((rows, HD), F32)
        value_grad = jnp.zeros((rows, HD), F32)
        for j in range(count):
            span = slice(j * rows, (j + 1) * rows)
            queries = qkv_ref[span, base : base + HD]
            back = back_ref[span, h * HD : (h + 1) * HD]
            stats = stats_ref[me ^ j]
            lse = stats[2 * h : 2 * h + 1, :]
            delta = stats[2 * h + 1 : 2 * h + 2, :]
            allowed = all_ref[:, span] >= own_order
            probs = jnp.exp(jnp.where(allowed, dot_nt(keys, queries) * SCALE - lse, -1e30))
            value_grad += dot_nn(probs.astype(BF16), back)
            probs_grad = dot_nt(values, back)
            score_grad = (probs * (probs_grad - delta)).astype(BF16)
            key_grad += dot_nn(score_grad, queries)
        grads = [adq_ref[:, (heads + h) * HD : (heads + h + 1) * HD]]
        grads += [unturn(key_grad * SCALE, cosine, sine).astype(BF16), value_grad.astype(BF16)]
        for j, grad in enumerate(grads):
            out_ref[:, base + j * HD : base + (j + 1) * HD] = grad


def attend_keys(me, qkv, back, stats, own_order, all_order, turns, adq, heads):
    rows = own_order.shape[0]
    total = qkv.shape[0]
    return pl.pallas_call(
        functools.partial(key_kernel, heads),
        in_specs=[SMEM_SPEC] + [VMEM_SPEC] * 7,
        out_shape=jax.ShapeDtypeStruct((rows, heads * 3 * HD), BF16),
        compiler_params=params(56),
        cost_estimate=pl.CostEstimate(
            flops=32 * heads * rows * total * HD, bytes_accessed=qkv.size * 2, transcendentals=heads * rows * total
        ),
        name="attend_keys",
    )(me, qkv, back, stats, own_order, all_order, turns, adq)


def dense_kernel(count, me_ref, cot_ref, *refs):
    pieces = refs[:count]
    out_ref, attended_ref = refs[count:]
    rows, cols = pieces[0].shape[0], out_ref.shape[0]

    @pl.when(pl.program_id(0) == 0)
    def _():
        for k, piece in enumerate(pieces):
            at = pl.ds(pl.multiple_of((me_ref[0] ^ k) * rows, rows), rows)
            attended_ref[at, :] = piece[...]

    out_ref[...] = dot_tn(attended_ref[...], cot_ref[...])


def dense_weight_grads(me, cot_all, pieces):
    total, width = cot_all.shape
    cols = pieces[0].shape[1]
    tile = 512
    whole = lambda a: pl.BlockSpec(a.shape, lambda i: (0, 0))
    return pl.pallas_call(
        functools.partial(dense_kernel, len(pieces)),
        grid=(width // tile,),
        in_specs=[SMEM_SPEC, pl.BlockSpec((total, tile), lambda i: (0, i))] + [whole(p) for p in pieces],
        out_specs=pl.BlockSpec((cols, tile), lambda i: (0, i)),
        out_shape=jax.ShapeDtypeStruct((cols, width), F32),
        scratch_shapes=[pltpu.VMEM((total, cols), BF16)],
        compiler_params=params(56),
        cost_estimate=pl.CostEstimate(
            flops=2 * total * width * cols, bytes_accessed=total * width * 2 + width * cols * 4, transcendentals=0
        ),
        name="dense_weight_grads",
    )(me, cot_all, *pieces)


def gelu_parts(hidden):
    size = jnp.abs(hidden) * (0.5 ** 0.5)
    t = 1.0 / (1.0 + 0.3275911 * size)
    bell = jnp.exp(-(size * size))
    series = 0.5 * 1.061405429
    for coefficient in (-1.453152027, 1.421413741, -0.284496736, 0.254829592):
        series = series * t + 0.5 * coefficient
    tail = series * t * bell
    phi = jnp.where(hidden >= 0, 1.0 - tail, tail)
    return hidden * phi, phi + hidden * bell * 0.3989422804014327


def gelu_kernel(xhat_ref, cot_ref, gains_ref, expand_ref, bias_ref, shrink_ref, active_ref, grad_ref):
    low = (xhat_ref[...].astype(F32) * gains_ref[2:3] + gains_ref[3:4]).astype(BF16)
    hidden = dot_nn(low, expand_ref[...]) + bias_ref[...]
    active, slope = gelu_parts(hidden)
    active_ref[...] = active.astype(BF16)
    grad_ref[...] = (dot_nt(cot_ref[...], shrink_ref[...]) * slope).astype(BF16)


def gelu_branch(xhat, cotangent, gains, expand, bias, shrink):
    rows, width = xhat.shape
    units = expand.shape[1]
    block = 256
    row_block = lambda w: pl.BlockSpec((block, w), lambda i: (i, 0))
    whole = lambda a: pl.BlockSpec(a.shape, lambda i: (0, 0))
    return pl.pallas_call(
        gelu_kernel,
        grid=(rows // block,),
        in_specs=[row_block(width), row_block(width), whole(gains), whole(expand), whole(bias), whole(shrink)],
        out_specs=[row_block(units), row_block(units)],
        out_shape=[jax.ShapeDtypeStruct((rows, units), BF16)] * 2,
        compiler_params=params(56),
        cost_estimate=pl.CostEstimate(
            flops=4 * rows * width * units, bytes_accessed=rows * (width + units) * 4, transcendentals=rows * units
        ),
        name="gelu_branch",
    )(xhat, cotangent, gains, expand, bias, shrink)


def norm_pull(back, xhat, scale, gain):
    weighted = back * gain
    mean = jnp.mean(weighted, axis=-1, keepdims=True)
    along = jnp.mean(weighted * xhat, axis=-1, keepdims=True)
    return (weighted - mean - xhat * along) * scale, jnp.sum(back * xhat, axis=0), jnp.sum(back, axis=0)


def on_device(
    layer_input,
    attn_norm_gain,
    attn_norm_bias,
    mlp_norm_gain,
    mlp_norm_bias,
    qkv_weight,
    qkv_bias,
    dense_weight,
    dense_bias,
    expand_weight,
    expand_bias,
    shrink_weight,
    shrink_bias,
    positions,
    pair_table,
    cotangent,
):
    count = lax.axis_size("ctx")
    me = lax.axis_index("ctx")
    rows = layer_input.shape[0]
    block_len = rows // 2
    heads = dense_weight.shape[0] // HD
    width = layer_input.shape[1]

    place = lax.axis_index("tp")
    me_table = me.reshape(1).astype(jnp.int32)
    cot_all = lax.all_gather(own_share(cotangent), ("ctx", "tp"), axis=0, tiled=True)

    pairs = pair_table[0]
    blocks = jnp.stack([pairs, 2 * count - 1 - pairs], axis=1).reshape(-1)
    offsets = jnp.arange(block_len, dtype=jnp.int32)
    order = (blocks[:, None] * block_len + offsets).reshape(-1)
    own_order = lax.dynamic_slice_in_dim(order, me * rows, rows, 0)[:, None]
    places = positions.reshape(2 * count, block_len)[blocks].reshape(-1).astype(F32)
    frequency = 10000.0 ** (-jnp.arange(0, ROT, 2, dtype=F32) / ROT)
    angles = frequency[:, None] * places[None, :]
    turns = split_turns(angles)
    own_turns = lax.dynamic_slice_in_dim(turns, me * rows, rows, 1)
    gains = jnp.stack([attn_norm_gain, attn_norm_bias, mlp_norm_gain, mlp_norm_bias]).astype(F32)
    cols = qkv_weight.shape[1]
    spare = -cols % 128
    weight_wide = jnp.pad(qkv_weight, ((0, 0), (0, spare)))
    bias_wide = jnp.pad(qkv_bias, (0, spare)).astype(F32)[None]
    beside = (turns, own_turns, own_order, dot_nt(cotangent, dense_weight).astype(BF16))
    pieces, (turns, own_turns, own_order, back_own) = gather_pieces(layer_input, beside)
    qkv, xhat_all = project(
        place,
        [me ^ k for k in range(count)],
        [[layer_input]] + pieces,
        gains,
        weight_wide,
        bias_wide,
        turns,
    )

    expand_bias_wide = expand_bias.astype(F32)[None]
    adq, stats = attend_queries(me_table, qkv, back_own, own_order, order[None, :], own_turns, heads)

    attended = adq[:, : heads * HD]
    input_wide = layer_input.astype(F32)
    average = jnp.mean(input_wide, axis=-1, keepdims=True)
    centered = input_wide - average
    scale = lax.rsqrt(jnp.mean(centered * centered, axis=-1, keepdims=True) + 1e-05)
    xhat = centered * scale
    got = swap(stats, "ctx", 1)
    back_all = dot_nt(after(cot_all, stats), dense_weight).astype(BF16)
    got, back_all, attended = tie(got, back_all, attended)
    pair = jnp.stack([stats, got])
    others = [swap(pair, "ctx", k) for k in range(2, count, 2)]
    partial = dot_nn(attended, dense_weight)
    others, partial, xhat = tie(others, partial, xhat)
    stats_all = jnp.concatenate([pair] + others, axis=0)

    attended, stats_all = tie(attended, stats_all)
    pieces = {k: swap(attended, "ctx", k) for k in [1] + list(range(2, count, 2))}
    qkv_grad = attend_keys(
        me_table, qkv, back_all, stats_all, own_order, order[None, :], own_turns, adq, heads
    )
    qkv_grad, xhat_all = tie(qkv_grad, xhat_all)
    qkv_grad_all = lax.all_gather(qkv_grad, "ctx", axis=0, tiled=True)
    active, hidden_grad = gelu_branch(
        xhat_all, cot_all, gains, expand_weight, expand_bias_wide, shrink_weight
    )

    pieces, active, hidden_grad = tie(pieces, active, hidden_grad)
    active_own = lax.dynamic_slice_in_dim(active, me * rows, rows, 0)
    hidden_grad_own = lax.dynamic_slice_in_dim(hidden_grad, me * rows, rows, 0)
    partial = partial + dot_nn(active_own, shrink_weight)
    attn_back = dot_nt(qkv_grad, qkv_weight)
    mlp_back = dot_nt(hidden_grad_own, expand_weight)
    attn_part, attn_gain_grad, attn_bias_grad = norm_pull(attn_back, xhat, scale, gains[0:1])
    mlp_part, mlp_gain_grad, mlp_bias_grad = norm_pull(mlp_back, xhat, scale, gains[2:3])
    norm_grads = jnp.stack([attn_gain_grad, attn_bias_grad, mlp_gain_grad, mlp_bias_grad])
    both = jnp.stack([partial, attn_part + mlp_part])
    both, norm_grads, active, hidden_grad = tie(both, norm_grads, active, hidden_grad)

    def normed_product(xhat_all, grad, gain, bias):
        sums = column_sums(grad)
        return gain[:, None] * dot_tn(xhat_all, grad) + bias[:, None] * sums[None, :], sums

    def far_pieces():
        far = yield {k: swap(pieces[k - 1], "ctx", 1) for k in range(3, count, 2)}
        pieces.update(far)

    def dense_product(cot_all):
        return dense_weight_grads(me_table, cot_all, [attended] + [pieces[k] for k in range(1, count)])

    (both, norm_grads, _), results = overlap(
        [sum_tp(both), sum_small(norm_grads, ("tp", "ctx")), far_pieces()],
        [
            (dot_tn, (active, cot_all)),
            (normed_product, (xhat_all, hidden_grad, gains[2], gains[3])),
            (dense_product, (cot_all,)),
            (column_sums, (cot_all,)),
        ],
    )
    shrink_grad, (expand_grad, expand_bias_grad), dense_grad, bias_grad = results
    qkv_weight_grad, qkv_bias_grad = normed_product(xhat_all, qkv_grad_all, gains[0], gains[1])
    bias_total = dense_bias.astype(F32) + shrink_bias.astype(F32)
    layer_output = (input_wide + both[0].astype(F32) + bias_total).astype(BF16)
    input_grad = cotangent.astype(F32) + both[1].astype(F32)
    return (
        layer_output,
        input_grad,
        norm_grads[0],
        norm_grads[1],
        norm_grads[2],
        norm_grads[3],
        qkv_weight_grad,
        qkv_bias_grad,
        dense_grad,
        bias_grad,
        expand_grad,
        expand_bias_grad,
        shrink_grad,
        bias_grad,
    )


def solution(mesh):
    placed = (
        P("ctx", None),
        P(),
        P(),
        P(),
        P(),
        P(None, "tp"),
        P("tp"),
        P("tp", None),
        P(),
        P(None, "tp"),
        P("tp"),
        P("tp", None),
        P(),
        P(),
        P(),
        P("ctx", None),
    )
    return jax.shard_map(
        on_device,
        mesh=mesh,
        in_specs=placed,
        out_specs=(
            P("ctx", None),
            P("ctx", None),
            P(),
            P(),
            P(),
            P(),
            P(None, "tp"),
            P("tp"),
            P("tp", None),
            P(),
            P(None, "tp"),
            P("tp"),
            P("tp", None),
            P(),
        ),
        check_vma=False,
    )
```

```python
import functools

import jax
import jax.numpy as jnp
from jax import lax
from jax.experimental import pallas as pl
from jax.experimental.pallas import tpu as pltpu
from jax.sharding import PartitionSpec as P

HD = 64
ROT = 16
SCALE = HD ** (-0.5)
F32 = jnp.float32
BF16 = jnp.bfloat16
MIB = 1024 * 1024


def dot_nn(left, right):
    return lax.dot_general(left, right, (((1,), (0,)), ((), ())), preferred_element_type=F32)


def dot_nt(left, right):
    return lax.dot_general(left, right, (((1,), (1,)), ((), ())), preferred_element_type=F32)


def dot_tn(left, right):
    return lax.dot_general(left, right, (((0,), (0,)), ((), ())), preferred_element_type=F32)


def swap(array, axis, bits):
    return lax.ppermute(array, axis, [(i, i ^ bits) for i in range(lax.axis_size(axis))])


def params(mib):
    return pltpu.CompilerParams(vmem_limit_bytes=mib * MIB)


VMEM_SPEC = pl.BlockSpec(memory_space=pltpu.VMEM)
SMEM_SPEC = pl.BlockSpec(memory_space=pltpu.SMEM)
ANY_SPEC = pl.BlockSpec(memory_space=pl.ANY)


def spread_ctx(own):
    count = lax.axis_size("ctx")
    pieces = [own]
    for k in range(1, count):
        pieces.append(swap(own, "ctx", k) if k % 2 == 0 else swap(pieces[k - 1], "ctx", 1))
    return pieces


def own_share(own):
    part = own.shape[0] // lax.axis_size("tp")
    return lax.dynamic_slice_in_dim(own, lax.axis_index("tp") * part, part, 0)


def gather_pieces(share, beside):
    count, shares = lax.axis_size("ctx"), lax.axis_size("tp")
    near = [1] + list(range(2, count, 2))
    far = list(range(3, count, 2))
    arrived = {(k, 0): swap(share, "ctx", k) for k in near}
    arrived, beside = tie(arrived, beside)
    levels = shares.bit_length() - 1

    def level(pieces, number):
        for k in pieces:
            for j in range(1, shares):
                if bin(j).count("1") == number:
                    low = j & -j
                    yield (k, j), swap(arrived[k, j ^ low], "tp", low)

    for stage in range(1, levels + 2):
        found = {}
        if stage == 1:
            found.update({(k, 0): swap(arrived[k - 1, 0], "ctx", 1) for k in far})
        found.update(level(near, stage))
        found.update(level(far, stage - 1))
        arrived.update(found)
    return [[arrived[k, j] for j in range(shares)] for k in range(1, count)], beside


def tie(*items):
    return lax.optimization_barrier(items if len(items) > 1 else items[0])


def after(array, other):
    return tie(array, other)[0]


def sum_tp(partial):
    shares = lax.axis_size("tp")
    place = lax.axis_index("tp")
    held = partial
    bit = 1
    while bit < shares:
        half = held.shape[1] // 2
        upper = (place // bit) % 2
        keep = lax.dynamic_slice_in_dim(held, upper * half, half, 1)
        give = lax.dynamic_slice_in_dim(held, (1 - upper) * half, half, 1)
        got = yield swap(give.astype(BF16), "tp", bit)
        held = keep + got.astype(F32)
        bit *= 2
    held = held.astype(BF16)
    while bit > 1:
        bit //= 2
        upper = (place // bit) % 2
        other = yield swap(held, "tp", bit)
        low = jnp.where(upper == 0, held, other)
        high = jnp.where(upper == 0, other, held)
        held = jnp.concatenate([low, high], axis=1)
    return held


def sum_small(partial, axes):
    held = partial
    for axis in axes:
        bit = 1
        while bit < lax.axis_size(axis):
            got = yield swap(held, axis, bit)
            held = held + got
            bit *= 2
    return held


def overlap(chains, steps):
    flying = {i: next(chain) for i, chain in enumerate(chains)}
    ends, results = {}, []

    def advance(arrived):
        for i, got in arrived.items():
            try:
                flying[i] = chains[i].send(got)
            except StopIteration as stop:
                ends[i] = stop.value
                del flying[i]

    operands = steps[0][1]
    for number, (run, _) in enumerate(steps):
        result = run(*operands)
        following = steps[number + 1][1] if number + 1 < len(steps) else ()
        following = following(ends) if callable(following) else following
        arrived, result, operands = tie(dict(flying), result, tuple(following))
        results.append(result)
        advance(arrived)
    while flying:
        advance(dict(flying))
    return [ends[i] for i in range(len(chains))], results


def column_sums(array):
    return dot_nn(jnp.ones((8, array.shape[0]), BF16), array)[0]


def rot_masks(shape):
    lane = lax.broadcasted_iota(jnp.int32, shape, 1) % HD
    return lane < ROT // 2, (lane >= ROT // 2) & (lane < ROT)


def rot_tables(compact):
    shape = (4 * (ROT // 2), 256)
    row, column = lax.broadcasted_iota(jnp.int32, shape, 0), lax.broadcasted_iota(jnp.int32, shape, 1)
    lane = column % HD
    hit = (lane < ROT) & (lane % (ROT // 2) == row % (ROT // 2)) & (column // 128 == row // ROT)
    both = dot_tn(compact, jnp.where(hit, 1.0, 0.0).astype(BF16))
    still = lax.broadcasted_iota(jnp.int32, (compact.shape[1], 128), 1) % HD >= ROT
    return jnp.where(still, 1.0, both[:, :128]), both[:, 128:]


def split_turns(angles):
    parts = []
    for table in (jnp.cos(angles), jnp.sin(angles)):
        high = lax.reduce_precision(table, 8, 7)
        parts += [high.astype(BF16), (table - high).astype(BF16)]
    return jnp.concatenate(parts, axis=0)


def project_kernel(groups, place_ref, *refs):
    parts = [refs[sum(groups[:g]) : sum(groups[: g + 1])] for g in range(len(groups))]
    gains_ref, weight_ref, bias_ref, turn_ref, out_ref, xhat_ref, x_ref, sems = refs[sum(groups) :]
    step = pl.program_id(0)
    steps = len(groups) // 2
    rows = x_ref.shape[1] // 2

    def load(g, act):
        for k in (2 * g, 2 * g + 1):
            upper = (place_ref[1] ^ k) & 1
            for j, part in enumerate(parts[k]):
                size = part.shape[0]
                at = upper * rows + ((place_ref[0] ^ j) * size if len(parts[k]) > 1 else 0)
                to = x_ref.at[g % 2, pl.ds(pl.multiple_of(at, size), size), :]
                act(pltpu.make_async_copy(part, to, sems.at[g % 2, k % 2, j]))

    for g in range(steps):

        @pl.when(step == g)
        def _():
            if g == 0:
                load(0, lambda copy: copy.start())
            if g + 1 < steps:
                load(g + 1, lambda copy: copy.start())
            load(g, lambda copy: copy.wait())

    values = x_ref[step % 2].astype(F32)
    average = jnp.mean(values, axis=-1, keepdims=True)
    centered = values - average
    spread = jnp.mean(centered * centered, axis=-1, keepdims=True)
    xhat = centered * lax.rsqrt(spread + 1e-05)
    xhat_ref[...] = xhat.astype(BF16)
    low = (xhat * gains_ref[0:1] + gains_ref[1:2]).astype(BF16)
    mixed = dot_nn(low, weight_ref[...]) + bias_ref[...]
    cosine, sine = rot_tables(turn_ref[...])
    lower, upper = rot_masks(sine.shape)
    back = jnp.where(lower, -sine, 0.0)
    ahead = jnp.where(upper, sine, 0.0)
    first = lax.broadcasted_iota(jnp.int32, sine.shape, 1) < HD
    mine = pl.ds(pl.multiple_of(((place_ref[1] // 2) ^ step) * 2 * rows, 2 * rows), 2 * rows)
    for col in range(mixed.shape[1] // 128):
        tile = mixed[:, col * 128 : (col + 1) * 128]
        turn = [(2 * col + j) % 3 < 2 for j in range(2)]
        turned = (
            tile * cosine + pltpu.roll(tile, 120, 1) * back + pltpu.roll(tile, 8, 1) * ahead
        )
        if not turn[0]:
            turned = jnp.where(first, tile, turned)
        if not turn[1]:
            turned = jnp.where(first, turned, tile)
        out_ref[mine, col * 128 : (col + 1) * 128] = turned.astype(BF16)


def project(place, me, pieces, gains, weight, bias, turns):
    total = turns.shape[1]
    groups = tuple(len(piece) for piece in pieces)
    parts = [part for piece in pieces for part in piece]
    rows, width = sum(part.shape[0] for part in pieces[0]), parts[0].shape[1]
    cols = weight.shape[1]
    whole = lambda a: pl.BlockSpec(a.shape, lambda i, place_ref: (0, 0))
    return pl.pallas_call(
        functools.partial(project_kernel, groups),
        grid_spec=pltpu.PrefetchScalarGridSpec(
            num_scalar_prefetch=1,
            grid=(len(pieces) // 2,),
            in_specs=[ANY_SPEC] * len(parts)
            + [whole(gains), whole(weight), whole(bias)]
            + [pl.BlockSpec((turns.shape[0], 2 * rows), lambda i, place_ref: (0, (place_ref[1] // 2) ^ i))],
            out_specs=[VMEM_SPEC, pl.BlockSpec((2 * rows, width), lambda i, place_ref: ((place_ref[1] // 2) ^ i, 0))],
            scratch_shapes=[
                pltpu.VMEM((2, 2 * rows, width), BF16),
                pltpu.SemaphoreType.DMA((2, 2, max(groups))),
            ],
        ),
        out_shape=[jax.ShapeDtypeStruct((total, cols), BF16), jax.ShapeDtypeStruct((total, width), BF16)],
        compiler_params=params(56),
        cost_estimate=pl.CostEstimate(
            flops=2 * total * width * cols, bytes_accessed=total * width * 4 + total * cols * 2, transcendentals=0
        ),
        name="project",
    )(jnp.stack([place, me]), *parts, gains, weight, bias, turns)


def unturn(grad, cosine, sine):
    half = ROT // 2
    rotated = grad[:, :ROT]
    turned = rotated * sine[:, :ROT]
    first = rotated[:, :half] * cosine[:, :half] + turned[:, half:]
    second = rotated[:, half:] * cosine[:, half:ROT] - turned[:, :half]
    return jnp.concatenate([first, second, grad[:, ROT:]], axis=1)


def query_kernel(heads, me_ref, qkv_ref, back_ref, own_ref, all_ref, turn_ref, out_ref, stats_ref):
    rows = back_ref.shape[0]
    mine = pl.ds(pl.multiple_of(me_ref[0] * rows, rows), rows)
    allowed = own_ref[...] >= all_ref[...]
    cosine, sine = rot_tables(turn_ref[...])
    columns = []
    for h in range(heads):
        base = h * 3 * HD
        queries = (qkv_ref[mine, base : base + HD].astype(F32) * SCALE).astype(BF16)
        keys = qkv_ref[:, base + HD : base + 2 * HD]
        values = qkv_ref[:, base + 2 * HD : base + 3 * HD]
        back = back_ref[:, h * HD : (h + 1) * HD]
        scores = jnp.where(allowed, dot_nt(queries, keys), -1e30)
        row_max = jnp.max(scores, axis=-1, keepdims=True)
        weights = jnp.exp(scores - row_max)
        total = jnp.sum(weights, axis=-1, keepdims=True)
        probs = weights * (1.0 / total)
        out_ref[:, h * HD : (h + 1) * HD] = dot_nn(probs.astype(BF16), values).astype(BF16)
        probs_grad = dot_nt(back, values)
        delta = jnp.sum(probs * probs_grad, axis=-1, keepdims=True)
        score_grad = (probs * (probs_grad - delta)).astype(BF16)
        query_grad = unturn(dot_nn(score_grad, keys) * SCALE, cosine, sine)
        out_ref[:, (heads + h) * HD : (heads + h + 1) * HD] = query_grad.astype(BF16)
        columns += [row_max + jnp.log(total), delta]
    lane = lax.broadcasted_iota(jnp.int32, (rows, 128), 1)
    table = jnp.zeros((rows, 128), F32)
    for j, column in enumerate(columns):
        table = jnp.where(lane == j, column, table)
    stats_ref[...] = table.T[: stats_ref.shape[0]]


def attend_queries(me, qkv, back, own_order, all_order, turns, heads):
    rows = back.shape[0]
    keys = qkv.shape[0]
    return pl.pallas_call(
        functools.partial(query_kernel, heads),
        in_specs=[SMEM_SPEC] + [VMEM_SPEC] * 5,
        out_shape=[
            jax.ShapeDtypeStruct((rows, 2 * heads * HD), BF16),
            jax.ShapeDtypeStruct((max(8, 2 * heads), rows), F32),
        ],
        compiler_params=params(56),
        cost_estimate=pl.CostEstimate(
            flops=32 * heads * rows * keys * HD, bytes_accessed=qkv.size * 2, transcendentals=heads * rows * keys
        ),
        name="attend_queries",
    )(me, qkv, back, own_order, all_order, turns)


def key_kernel(heads, me_ref, qkv_ref, back_ref, stats_ref, own_ref, all_ref, turn_ref, adq_ref, out_ref):
    rows = out_ref.shape[0]
    count = qkv_ref.shape[0] // rows
    me = me_ref[0]
    mine = pl.ds(pl.multiple_of(me * rows, rows), rows)
    own_order = own_ref[...]
    cosine, sine = rot_tables(turn_ref[...])
    for h in range(heads):
        base = h * 3 * HD
        keys = (qkv_ref[mine, base + HD : base + 2 * HD].astype(F32) * SCALE).astype(BF16)
        values = qkv_ref[mine, base + 2 * HD : base + 3 * HD]
        key_grad = jnp.zeros((rows, HD), F32)
        value_grad = jnp.zeros((rows, HD), F32)
        for j in range(count):
            span = slice(j * rows, (j + 1) * rows)
            queries = qkv_ref[span, base : base + HD]
            back = back_ref[span, h * HD : (h + 1) * HD]
            stats = stats_ref[me ^ j]
            lse = stats[2 * h : 2 * h + 1, :]
            delta = stats[2 * h + 1 : 2 * h + 2, :]
            allowed = all_ref[:, span] >= own_order
            probs = jnp.exp(jnp.where(allowed, dot_nt(keys, queries) - lse, -1e30))
            value_grad += dot_nn(probs.astype(BF16), back)
            probs_grad = dot_nt(values, back)
            score_grad = (probs * (probs_grad - delta)).astype(BF16)
            key_grad += dot_nn(score_grad, queries)
        grads = [adq_ref[:, (heads + h) * HD : (heads + h + 1) * HD]]
        grads += [unturn(key_grad * SCALE, cosine, sine).astype(BF16), value_grad.astype(BF16)]
        for j, grad in enumerate(grads):
            out_ref[:, base + j * HD : base + (j + 1) * HD] = grad


def attend_keys(me, qkv, back, stats, own_order, all_order, turns, adq, heads):
    rows = own_order.shape[0]
    total = qkv.shape[0]
    return pl.pallas_call(
        functools.partial(key_kernel, heads),
        in_specs=[SMEM_SPEC] + [VMEM_SPEC] * 7,
        out_shape=jax.ShapeDtypeStruct((rows, heads * 3 * HD), BF16),
        compiler_params=params(56),
        cost_estimate=pl.CostEstimate(
            flops=32 * heads * rows * total * HD, bytes_accessed=qkv.size * 2, transcendentals=heads * rows * total
        ),
        name="attend_keys",
    )(me, qkv, back, stats, own_order, all_order, turns, adq)


def dense_kernel(count, me_ref, cot_ref, *refs):
    pieces = refs[:count]
    out_ref, attended_ref = refs[count:]
    rows, cols = pieces[0].shape[0], out_ref.shape[0]

    @pl.when(pl.program_id(0) == 0)
    def _():
        for k, piece in enumerate(pieces):
            at = pl.ds(pl.multiple_of((me_ref[0] ^ k) * rows, rows), rows)
            attended_ref[at, :] = piece[...]

    out_ref[...] = dot_tn(attended_ref[...], cot_ref[...])


def dense_weight_grads(me, cot_all, pieces):
    total, width = cot_all.shape
    cols = pieces[0].shape[1]
    tile = 512
    whole = lambda a: pl.BlockSpec(a.shape, lambda i: (0, 0))
    return pl.pallas_call(
        functools.partial(dense_kernel, len(pieces)),
        grid=(width // tile,),
        in_specs=[SMEM_SPEC, pl.BlockSpec((total, tile), lambda i: (0, i))] + [whole(p) for p in pieces],
        out_specs=pl.BlockSpec((cols, tile), lambda i: (0, i)),
        out_shape=jax.ShapeDtypeStruct((cols, width), F32),
        scratch_shapes=[pltpu.VMEM((total, cols), BF16)],
        compiler_params=params(56),
        cost_estimate=pl.CostEstimate(
            flops=2 * total * width * cols, bytes_accessed=total * width * 2 + width * cols * 4, transcendentals=0
        ),
        name="dense_weight_grads",
    )(me, cot_all, *pieces)


def gelu_parts(hidden):
    size = jnp.abs(hidden) * (0.5 ** 0.5)
    t = 1.0 / (1.0 + 0.3275911 * size)
    bell = jnp.exp(-(size * size))
    series = 0.5 * 1.061405429
    for coefficient in (-1.453152027, 1.421413741, -0.284496736, 0.254829592):
        series = series * t + 0.5 * coefficient
    tail = series * t * bell
    phi = jnp.where(hidden >= 0, 1.0 - tail, tail)
    return hidden * phi, phi + hidden * bell * 0.3989422804014327


def gelu_kernel(xhat_ref, cot_ref, gains_ref, expand_ref, bias_ref, shrink_ref, active_ref, grad_ref):
    low = (xhat_ref[...].astype(F32) * gains_ref[2:3] + gains_ref[3:4]).astype(BF16)
    hidden = dot_nn(low, expand_ref[...]) + bias_ref[...]
    active, slope = gelu_parts(hidden)
    active_ref[...] = active.astype(BF16)
    grad_ref[...] = (dot_nt(cot_ref[...], shrink_ref[...]) * slope).astype(BF16)


def gelu_branch(xhat, cotangent, gains, expand, bias, shrink):
    rows, width = xhat.shape
    units = expand.shape[1]
    block = 256
    row_block = lambda w: pl.BlockSpec((block, w), lambda i: (i, 0))
    whole = lambda a: pl.BlockSpec(a.shape, lambda i: (0, 0))
    return pl.pallas_call(
        gelu_kernel,
        grid=(rows // block,),
        in_specs=[row_block(width), row_block(width), whole(gains), whole(expand), whole(bias), whole(shrink)],
        out_specs=[row_block(units), row_block(units)],
        out_shape=[jax.ShapeDtypeStruct((rows, units), BF16)] * 2,
        compiler_params=params(56),
        cost_estimate=pl.CostEstimate(
            flops=4 * rows * width * units, bytes_accessed=rows * (width + units) * 4, transcendentals=rows * units
        ),
        name="gelu_branch",
    )(xhat, cotangent, gains, expand, bias, shrink)


def norm_pull(back, xhat, scale, gain):
    weighted = back * gain
    mean = jnp.mean(weighted, axis=-1, keepdims=True)
    along = jnp.mean(weighted * xhat, axis=-1, keepdims=True)
    return (weighted - mean - xhat * along) * scale, jnp.sum(back * xhat, axis=0), jnp.sum(back, axis=0)


def on_device(
    layer_input,
    attn_norm_gain,
    attn_norm_bias,
    mlp_norm_gain,
    mlp_norm_bias,
    qkv_weight,
    qkv_bias,
    dense_weight,
    dense_bias,
    expand_weight,
    expand_bias,
    shrink_weight,
    shrink_bias,
    positions,
    pair_table,
    cotangent,
):
    count = lax.axis_size("ctx")
    me = lax.axis_index("ctx")
    rows = layer_input.shape[0]
    block_len = rows // 2
    heads = dense_weight.shape[0] // HD
    width = layer_input.shape[1]

    place = lax.axis_index("tp")
    me_table = me.reshape(1).astype(jnp.int32)
    share = own_share(layer_input)
    cot_share = own_share(after(cotangent, share))
    cot_all = lax.all_gather(cot_share, ("ctx", "tp"), axis=0, tiled=True)

    pairs = pair_table[0]
    blocks = jnp.stack([pairs, 2 * count - 1 - pairs], axis=1).reshape(-1)
    offsets = jnp.arange(block_len, dtype=jnp.int32)
    order = (blocks[:, None] * block_len + offsets).reshape(-1)
    own_order = lax.dynamic_slice_in_dim(order, me * rows, rows, 0)[:, None]
    places = positions.reshape(2 * count, block_len)[blocks].reshape(-1).astype(F32)
    frequency = 10000.0 ** (-jnp.arange(0, ROT, 2, dtype=F32) / ROT)
    angles = frequency[:, None] * places[None, :]
    turns = split_turns(angles)
    own_turns = lax.dynamic_slice_in_dim(turns, me * rows, rows, 1)
    gains = jnp.stack([attn_norm_gain, attn_norm_bias, mlp_norm_gain, mlp_norm_bias]).astype(F32)
    cols = qkv_weight.shape[1]
    spare = -cols % 128
    weight_wide = jnp.pad(qkv_weight, ((0, 0), (0, spare)))
    bias_wide = jnp.pad(qkv_bias, (0, spare)).astype(F32)[None]
    beside = (turns, own_turns, own_order, dot_nt(cotangent, dense_weight).astype(BF16))
    pieces, (turns, own_turns, own_order, back_own) = gather_pieces(share, beside)
    qkv, xhat_all = project(
        place,
        me,
        [[layer_input]] + pieces,
        gains,
        weight_wide,
        bias_wide,
        turns,
    )

    expand_bias_wide = expand_bias.astype(F32)[None]
    adq, stats = attend_queries(me_table, qkv, back_own, own_order, order[None, :], own_turns, heads)

    attended = adq[:, : heads * HD]
    input_wide = layer_input.astype(F32)
    average = jnp.mean(input_wide, axis=-1, keepdims=True)
    centered = input_wide - average
    scale = lax.rsqrt(jnp.mean(centered * centered, axis=-1, keepdims=True) + 1e-05)
    xhat = centered * scale
    got = swap(stats, "ctx", 1)
    back_all = dot_nt(after(cot_all, stats), dense_weight).astype(BF16)
    got, back_all, attended = tie(got, back_all, attended)
    pair = jnp.stack([stats, got])
    others = [swap(pair, "ctx", k) for k in range(2, count, 2)]
    partial = dot_nn(attended, dense_weight)
    others, partial, xhat = tie(others, partial, xhat)
    stats_all = jnp.concatenate([pair] + others, axis=0)

    attended, stats_all = tie(attended, stats_all)
    pieces = {k: swap(attended, "ctx", k) for k in [1] + list(range(2, count, 2))}
    qkv_grad = attend_keys(
        me_table, qkv, back_all, stats_all, own_order, order[None, :], own_turns, adq, heads
    )
    qkv_grad_all = lax.all_gather(qkv_grad, "ctx", axis=0, tiled=True)
    pieces, qkv_grad, xhat_all = tie(pieces, qkv_grad, xhat_all)
    far = {k: swap(pieces[k - 1], "ctx", 1) for k in range(3, count, 2)}
    active, hidden_grad = gelu_branch(
        xhat_all, cot_all, gains, expand_weight, expand_bias_wide, shrink_weight
    )

    far, active, hidden_grad = tie(far, active, hidden_grad)
    pieces.update(far)
    active_own = lax.dynamic_slice_in_dim(active, me * rows, rows, 0)
    hidden_grad_own = lax.dynamic_slice_in_dim(hidden_grad, me * rows, rows, 0)
    partial = partial + dot_nn(active_own, shrink_weight)
    attn_back = dot_nt(qkv_grad, qkv_weight)
    mlp_back = dot_nt(hidden_grad_own, expand_weight)
    attn_part, attn_gain_grad, attn_bias_grad = norm_pull(attn_back, xhat, scale, gains[0:1])
    mlp_part, mlp_gain_grad, mlp_bias_grad = norm_pull(mlp_back, xhat, scale, gains[2:3])
    norm_grads = jnp.stack([attn_gain_grad, attn_bias_grad, mlp_gain_grad, mlp_bias_grad])
    own_sums = column_sums(qkv_grad).reshape(-1, HD)
    both = jnp.stack([partial, attn_part + mlp_part])
    both, norm_grads, own_sums, active, hidden_grad = tie(both, norm_grads, own_sums, active, hidden_grad)

    def normed_product(xhat_all, grad, gain, bias):
        sums = column_sums(grad)
        return gain[:, None] * dot_tn(xhat_all, grad) + bias[:, None] * sums[None, :], sums

    def qkv_product(xhat_all, grad, sums):
        sums = column_sums(grad) if sums is None else sums.reshape(-1)
        return gains[0][:, None] * dot_tn(xhat_all, grad) + gains[1][:, None] * sums[None, :]

    def dense_product(cot_all):
        return dense_weight_grads(me_table, cot_all, [attended] + [pieces[k] for k in range(1, count)])

    (both, norm_grads, qkv_bias_grad), results = overlap(
        [sum_tp(both), sum_small(norm_grads, ("tp", "ctx")), sum_small(own_sums, ("ctx",))],
        [
            (dot_tn, (active, cot_all)),
            (normed_product, (xhat_all, hidden_grad, gains[2], gains[3])),
            (dense_product, (cot_all,)),
            (column_sums, (cot_all,)),
            (qkv_product, lambda ends: (xhat_all, qkv_grad_all, ends.get(2))),
        ],
    )
    shrink_grad, (expand_grad, expand_bias_grad), dense_grad, bias_grad, qkv_weight_grad = results
    qkv_bias_grad = qkv_bias_grad.reshape(-1)
    bias_total = dense_bias.astype(F32) + shrink_bias.astype(F32)
    layer_output = (input_wide + both[0].astype(F32) + bias_total).astype(BF16)
    input_grad = cotangent.astype(F32) + both[1].astype(F32)
    return (
        layer_output,
        input_grad,
        norm_grads[0],
        norm_grads[1],
        norm_grads[2],
        norm_grads[3],
        qkv_weight_grad,
        qkv_bias_grad,
        dense_grad,
        bias_grad,
        expand_grad,
        expand_bias_grad,
        shrink_grad,
        bias_grad,
    )


def solution(mesh):
    placed = (
        P("ctx", None),
        P(),
        P(),
        P(),
        P(),
        P(None, "tp"),
        P("tp"),
        P("tp", None),
        P(),
        P(None, "tp"),
        P("tp"),
        P("tp", None),
        P(),
        P(),
        P(),
        P("ctx", None),
    )
    return jax.shard_map(
        on_device,
        mesh=mesh,
        in_specs=placed,
        out_specs=(
            P("ctx", None),
            P("ctx", None),
            P(),
            P(),
            P(),
            P(),
            P(None, "tp"),
            P("tp"),
            P("tp", None),
            P(),
            P(None, "tp"),
            P("tp"),
            P("tp", None),
            P(),
        ),
        check_vma=False,
    )
```

```python
import functools

import jax
import jax.numpy as jnp
from jax import lax
from jax.experimental import pallas as pl
from jax.experimental.pallas import tpu as pltpu
from jax.sharding import PartitionSpec as P

HD = 64
ROT = 16
SCALE = HD ** (-0.5)
F32 = jnp.float32
BF16 = jnp.bfloat16
MIB = 1024 * 1024


def dot_nn(left, right):
    return lax.dot_general(left, right, (((1,), (0,)), ((), ())), preferred_element_type=F32)


def dot_nt(left, right):
    return lax.dot_general(left, right, (((1,), (1,)), ((), ())), preferred_element_type=F32)


def dot_tn(left, right):
    return lax.dot_general(left, right, (((0,), (0,)), ((), ())), preferred_element_type=F32)


def swap(array, axis, bits):
    return lax.ppermute(array, axis, [(i, i ^ bits) for i in range(lax.axis_size(axis))])


def params(mib):
    return pltpu.CompilerParams(vmem_limit_bytes=mib * MIB)


VMEM_SPEC = pl.BlockSpec(memory_space=pltpu.VMEM)
SMEM_SPEC = pl.BlockSpec(memory_space=pltpu.SMEM)
ANY_SPEC = pl.BlockSpec(memory_space=pl.ANY)


def spread_ctx(own):
    count = lax.axis_size("ctx")
    pieces = [own]
    for k in range(1, count):
        pieces.append(swap(own, "ctx", k) if k % 2 == 0 else swap(pieces[k - 1], "ctx", 1))
    return pieces


def own_share(own):
    part = own.shape[0] // lax.axis_size("tp")
    return lax.dynamic_slice_in_dim(own, lax.axis_index("tp") * part, part, 0)


def gather_pieces(share, beside):
    count, shares = lax.axis_size("ctx"), lax.axis_size("tp")
    near = [1] + list(range(2, count, 2))
    far = list(range(3, count, 2))
    arrived = {(k, 0): swap(share, "ctx", k) for k in near}
    arrived, beside = tie(arrived, beside)
    levels = shares.bit_length() - 1

    def level(pieces, number):
        for k in pieces:
            for j in range(1, shares):
                if bin(j).count("1") == number:
                    low = j & -j
                    yield (k, j), swap(arrived[k, j ^ low], "tp", low)

    for stage in range(1, levels + 2):
        found = {}
        if stage == 1:
            found.update({(k, 0): swap(arrived[k - 1, 0], "ctx", 1) for k in far})
        found.update(level(near, stage))
        found.update(level(far, stage - 1))
        arrived.update(found)
    return [[arrived[k, j] for j in range(shares)] for k in range(1, count)], beside


def tie(*items):
    return lax.optimization_barrier(items if len(items) > 1 else items[0])


def after(array, other):
    return tie(array, other)[0]


def sum_tp(partial):
    shares = lax.axis_size("tp")
    place = lax.axis_index("tp")
    held = partial
    bit = 1
    while bit < shares:
        half = held.shape[1] // 2
        upper = (place // bit) % 2
        keep = lax.dynamic_slice_in_dim(held, upper * half, half, 1)
        give = lax.dynamic_slice_in_dim(held, (1 - upper) * half, half, 1)
        got = yield swap(give.astype(BF16), "tp", bit)
        held = keep + got.astype(F32)
        bit *= 2
    held = held.astype(BF16)
    while bit > 1:
        bit //= 2
        upper = (place // bit) % 2
        other = yield swap(held, "tp", bit)
        low = jnp.where(upper == 0, held, other)
        high = jnp.where(upper == 0, other, held)
        held = jnp.concatenate([low, high], axis=1)
    return held


def sum_small(partial, axes):
    held = partial
    for axis in axes:
        bit = 1
        while bit < lax.axis_size(axis):
            got = yield swap(held, axis, bit)
            held = held + got
            bit *= 2
    return held


def overlap(chains, steps):
    flying = {i: next(chain) for i, chain in enumerate(chains)}
    ends, results = {}, []

    def advance(arrived):
        for i, got in arrived.items():
            try:
                flying[i] = chains[i].send(got)
            except StopIteration as stop:
                ends[i] = stop.value
                del flying[i]

    operands = steps[0][1]
    for number, (run, _) in enumerate(steps):
        result = run(*operands)
        following = steps[number + 1][1] if number + 1 < len(steps) else ()
        following = following(ends) if callable(following) else following
        arrived, result, operands = tie(dict(flying), result, tuple(following))
        results.append(result)
        advance(arrived)
    while flying:
        advance(dict(flying))
    return [ends[i] for i in range(len(chains))], results


def column_sums(array):
    return dot_nn(jnp.ones((8, array.shape[0]), BF16), array)[0]


def rot_masks(shape):
    lane = lax.broadcasted_iota(jnp.int32, shape, 1) % HD
    return lane < ROT // 2, (lane >= ROT // 2) & (lane < ROT)


def rot_tables(compact):
    shape = (4 * (ROT // 2), 256)
    row, column = lax.broadcasted_iota(jnp.int32, shape, 0), lax.broadcasted_iota(jnp.int32, shape, 1)
    lane = column % HD
    hit = (lane < ROT) & (lane % (ROT // 2) == row % (ROT // 2)) & (column // 128 == row // ROT)
    both = dot_tn(compact, jnp.where(hit, 1.0, 0.0).astype(BF16))
    still = lax.broadcasted_iota(jnp.int32, (compact.shape[1], 128), 1) % HD >= ROT
    return jnp.where(still, 1.0, both[:, :128]), both[:, 128:]


def split_turns(angles):
    parts = []
    for table in (jnp.cos(angles), jnp.sin(angles)):
        high = lax.reduce_precision(table, 8, 7)
        parts += [high.astype(BF16), (table - high).astype(BF16)]
    return jnp.concatenate(parts, axis=0)


def project_kernel(groups, place_ref, *refs):
    parts = [refs[sum(groups[:g]) : sum(groups[: g + 1])] for g in range(len(groups))]
    gains_ref, weight_ref, bias_ref, turn_ref, out_ref, xhat_ref, x_ref, sems = refs[sum(groups) :]
    step = pl.program_id(0)
    steps = len(groups) // 2
    rows = x_ref.shape[1] // 2

    def load(g, act):
        for k in (2 * g, 2 * g + 1):
            upper = (place_ref[1] ^ k) & 1
            for j, part in enumerate(parts[k]):
                size = part.shape[0]
                at = upper * rows + ((place_ref[0] ^ j) * size if len(parts[k]) > 1 else 0)
                to = x_ref.at[g % 2, pl.ds(pl.multiple_of(at, size), size), :]
                act(pltpu.make_async_copy(part, to, sems.at[g % 2, k % 2, j]))

    for g in range(steps):

        @pl.when(step == g)
        def _():
            if g == 0:
                load(0, lambda copy: copy.start())
            if g + 1 < steps:
                load(g + 1, lambda copy: copy.start())
            load(g, lambda copy: copy.wait())

    values = x_ref[step % 2].astype(F32)
    average = jnp.mean(values, axis=-1, keepdims=True)
    centered = values - average
    spread = jnp.mean(centered * centered, axis=-1, keepdims=True)
    xhat = centered * lax.rsqrt(spread + 1e-05)
    xhat_ref[...] = xhat.astype(BF16)
    low = (xhat * gains_ref[0:1] + gains_ref[1:2]).astype(BF16)
    mixed = dot_nn(low, weight_ref[...]) + bias_ref[...]
    cosine, sine = rot_tables(turn_ref[...])
    lower, upper = rot_masks(sine.shape)
    back = jnp.where(lower, -sine, 0.0)
    ahead = jnp.where(upper, sine, 0.0)
    first = lax.broadcasted_iota(jnp.int32, sine.shape, 1) < HD
    mine = pl.ds(pl.multiple_of(((place_ref[1] // 2) ^ step) * 2 * rows, 2 * rows), 2 * rows)
    for col in range(mixed.shape[1] // 128):
        tile = mixed[:, col * 128 : (col + 1) * 128]
        turn = [(2 * col + j) % 3 < 2 for j in range(2)]
        turned = (
            tile * cosine + pltpu.roll(tile, 120, 1) * back + pltpu.roll(tile, 8, 1) * ahead
        )
        if not turn[0]:
            turned = jnp.where(first, tile, turned)
        if not turn[1]:
            turned = jnp.where(first, turned, tile)
        out_ref[mine, col * 128 : (col + 1) * 128] = turned.astype(BF16)


def project(place, me, pieces, gains, weight, bias, turns):
    total = turns.shape[1]
    groups = tuple(len(piece) for piece in pieces)
    parts = [part for piece in pieces for part in piece]
    rows, width = sum(part.shape[0] for part in pieces[0]), parts[0].shape[1]
    cols = weight.shape[1]
    whole = lambda a: pl.BlockSpec(a.shape, lambda i, place_ref: (0, 0))
    return pl.pallas_call(
        functools.partial(project_kernel, groups),
        grid_spec=pltpu.PrefetchScalarGridSpec(
            num_scalar_prefetch=1,
            grid=(len(pieces) // 2,),
            in_specs=[ANY_SPEC] * len(parts)
            + [whole(gains), whole(weight), whole(bias)]
            + [pl.BlockSpec((turns.shape[0], 2 * rows), lambda i, place_ref: (0, (place_ref[1] // 2) ^ i))],
            out_specs=[VMEM_SPEC, pl.BlockSpec((2 * rows, width), lambda i, place_ref: ((place_ref[1] // 2) ^ i, 0))],
            scratch_shapes=[
                pltpu.VMEM((2, 2 * rows, width), BF16),
                pltpu.SemaphoreType.DMA((2, 2, max(groups))),
            ],
        ),
        out_shape=[jax.ShapeDtypeStruct((total, cols), BF16), jax.ShapeDtypeStruct((total, width), BF16)],
        compiler_params=params(56),
        cost_estimate=pl.CostEstimate(
            flops=2 * total * width * cols, bytes_accessed=total * width * 4 + total * cols * 2, transcendentals=0
        ),
        name="project",
    )(jnp.stack([place, me]), *parts, gains, weight, bias, turns)


def unturn(grad, cosine, sine):
    half = ROT // 2
    rotated = grad[:, :ROT]
    turned = rotated * sine[:, :ROT]
    first = rotated[:, :half] * cosine[:, :half] + turned[:, half:]
    second = rotated[:, half:] * cosine[:, half:ROT] - turned[:, :half]
    return jnp.concatenate([first, second, grad[:, ROT:]], axis=1)


def query_kernel(heads, me_ref, qkv_ref, back_ref, own_ref, all_ref, turn_ref, out_ref, stats_ref):
    rows = back_ref.shape[0]
    mine = pl.ds(pl.multiple_of(me_ref[0] * rows, rows), rows)
    allowed = own_ref[...] >= all_ref[...]
    cosine, sine = rot_tables(turn_ref[...])
    columns = []
    for h in range(heads):
        base = h * 3 * HD
        queries = (qkv_ref[mine, base : base + HD].astype(F32) * SCALE).astype(BF16)
        keys = qkv_ref[:, base + HD : base + 2 * HD]
        values = qkv_ref[:, base + 2 * HD : base + 3 * HD]
        back = back_ref[:, h * HD : (h + 1) * HD]
        scores = jnp.where(allowed, dot_nt(queries, keys), -1e30)
        probs_grad = dot_nt(back, values)
        row_max = jnp.max(scores, axis=-1, keepdims=True)
        weights = jnp.exp(scores - row_max)
        total = jnp.sum(weights, axis=-1, keepdims=True)
        inverse = 1.0 / total
        probs = weights * inverse
        out_ref[:, h * HD : (h + 1) * HD] = dot_nn(probs.astype(BF16), values).astype(BF16)
        delta = jnp.sum(weights * probs_grad, axis=-1, keepdims=True) * inverse
        score_grad = (probs * (probs_grad - delta)).astype(BF16)
        query_grad = unturn(dot_nn(score_grad, keys) * SCALE, cosine, sine)
        out_ref[:, (heads + h) * HD : (heads + h + 1) * HD] = query_grad.astype(BF16)
        columns += [row_max + jnp.log(total), delta]
    lane = lax.broadcasted_iota(jnp.int32, (rows, 128), 1)
    table = jnp.zeros((rows, 128), F32)
    for j, column in enumerate(columns):
        table = jnp.where(lane == j, column, table)
    stats_ref[...] = table.T[: stats_ref.shape[0]]


def attend_queries(me, qkv, back, own_order, all_order, turns, heads):
    rows = back.shape[0]
    keys = qkv.shape[0]
    return pl.pallas_call(
        functools.partial(query_kernel, heads),
        in_specs=[SMEM_SPEC] + [VMEM_SPEC] * 5,
        out_shape=[
            jax.ShapeDtypeStruct((rows, 2 * heads * HD), BF16),
            jax.ShapeDtypeStruct((max(8, 2 * heads), rows), F32),
        ],
        compiler_params=params(56),
        cost_estimate=pl.CostEstimate(
            flops=32 * heads * rows * keys * HD, bytes_accessed=qkv.size * 2, transcendentals=heads * rows * keys
        ),
        name="attend_queries",
    )(me, qkv, back, own_order, all_order, turns)


def key_kernel(heads, me_ref, qkv_ref, back_ref, stats_ref, own_ref, all_ref, turn_ref, adq_ref, out_ref):
    rows = out_ref.shape[0]
    count = qkv_ref.shape[0] // rows
    me = me_ref[0]
    mine = pl.ds(pl.multiple_of(me * rows, rows), rows)
    own_order = own_ref[...]
    cosine, sine = rot_tables(turn_ref[...])
    for h in range(heads):
        base = h * 3 * HD
        keys = (qkv_ref[mine, base + HD : base + 2 * HD].astype(F32) * SCALE).astype(BF16)
        values = qkv_ref[mine, base + 2 * HD : base + 3 * HD]
        key_grad = jnp.zeros((rows, HD), F32)
        value_grad = jnp.zeros((rows, HD), F32)
        for j in range(count):
            span = slice(j * rows, (j + 1) * rows)
            queries = qkv_ref[span, base : base + HD]
            back = back_ref[span, h * HD : (h + 1) * HD]
            stats = stats_ref[me ^ j]
            lse = stats[2 * h : 2 * h + 1, :]
            delta = stats[2 * h + 1 : 2 * h + 2, :]
            allowed = all_ref[:, span] >= own_order
            probs = jnp.exp(jnp.where(allowed, dot_nt(keys, queries) - lse, -1e30))
            value_grad += dot_nn(probs.astype(BF16), back)
            probs_grad = dot_nt(values, back)
            score_grad = (probs * (probs_grad - delta)).astype(BF16)
            key_grad += dot_nn(score_grad, queries)
        grads = [adq_ref[:, (heads + h) * HD : (heads + h + 1) * HD]]
        grads += [unturn(key_grad * SCALE, cosine, sine).astype(BF16), value_grad.astype(BF16)]
        for j, grad in enumerate(grads):
            out_ref[:, base + j * HD : base + (j + 1) * HD] = grad


def attend_keys(me, qkv, back, stats, own_order, all_order, turns, adq, heads):
    rows = own_order.shape[0]
    total = qkv.shape[0]
    return pl.pallas_call(
        functools.partial(key_kernel, heads),
        in_specs=[SMEM_SPEC] + [VMEM_SPEC] * 7,
        out_shape=jax.ShapeDtypeStruct((rows, heads * 3 * HD), BF16),
        compiler_params=params(56),
        cost_estimate=pl.CostEstimate(
            flops=32 * heads * rows * total * HD, bytes_accessed=qkv.size * 2, transcendentals=heads * rows * total
        ),
        name="attend_keys",
    )(me, qkv, back, stats, own_order, all_order, turns, adq)


def dense_kernel(count, me_ref, cot_ref, *refs):
    pieces = refs[:count]
    out_ref, attended_ref = refs[count:]
    rows, cols = pieces[0].shape[0], out_ref.shape[0]

    @pl.when(pl.program_id(0) == 0)
    def _():
        for k, piece in enumerate(pieces):
            at = pl.ds(pl.multiple_of((me_ref[0] ^ k) * rows, rows), rows)
            attended_ref[at, :] = piece[...]

    out_ref[...] = dot_tn(attended_ref[...], cot_ref[...])


def dense_weight_grads(me, cot_all, pieces):
    total, width = cot_all.shape
    cols = pieces[0].shape[1]
    tile = 512
    whole = lambda a: pl.BlockSpec(a.shape, lambda i: (0, 0))
    return pl.pallas_call(
        functools.partial(dense_kernel, len(pieces)),
        grid=(width // tile,),
        in_specs=[SMEM_SPEC, pl.BlockSpec((total, tile), lambda i: (0, i))] + [whole(p) for p in pieces],
        out_specs=pl.BlockSpec((cols, tile), lambda i: (0, i)),
        out_shape=jax.ShapeDtypeStruct((cols, width), F32),
        scratch_shapes=[pltpu.VMEM((total, cols), BF16)],
        compiler_params=params(56),
        cost_estimate=pl.CostEstimate(
            flops=2 * total * width * cols, bytes_accessed=total * width * 2 + width * cols * 4, transcendentals=0
        ),
        name="dense_weight_grads",
    )(me, cot_all, *pieces)


def gelu_parts(hidden):
    size = jnp.abs(hidden) * (0.5 ** 0.5)
    t = 1.0 / (1.0 + 0.3275911 * size)
    bell = jnp.exp(-(size * size))
    series = 0.5 * 1.061405429
    for coefficient in (-1.453152027, 1.421413741, -0.284496736, 0.254829592):
        series = series * t + 0.5 * coefficient
    tail = series * t * bell
    phi = jnp.where(hidden >= 0, 1.0 - tail, tail)
    return hidden * phi, phi + hidden * bell * 0.3989422804014327


def gelu_kernel(xhat_ref, cot_ref, gains_ref, expand_ref, bias_ref, shrink_ref, active_ref, grad_ref):
    low = (xhat_ref[...].astype(F32) * gains_ref[2:3] + gains_ref[3:4]).astype(BF16)
    hidden = dot_nn(low, expand_ref[...]) + bias_ref[...]
    active, slope = gelu_parts(hidden)
    active_ref[...] = active.astype(BF16)
    grad_ref[...] = (dot_nt(cot_ref[...], shrink_ref[...]) * slope).astype(BF16)


def gelu_branch(xhat, cotangent, gains, expand, bias, shrink):
    rows, width = xhat.shape
    units = expand.shape[1]
    block = 256
    row_block = lambda w: pl.BlockSpec((block, w), lambda i: (i, 0))
    whole = lambda a: pl.BlockSpec(a.shape, lambda i: (0, 0))
    return pl.pallas_call(
        gelu_kernel,
        grid=(rows // block,),
        in_specs=[row_block(width), row_block(width), whole(gains), whole(expand), whole(bias), whole(shrink)],
        out_specs=[row_block(units), row_block(units)],
        out_shape=[jax.ShapeDtypeStruct((rows, units), BF16)] * 2,
        compiler_params=params(56),
        cost_estimate=pl.CostEstimate(
            flops=4 * rows * width * units, bytes_accessed=rows * (width + units) * 4, transcendentals=rows * units
        ),
        name="gelu_branch",
    )(xhat, cotangent, gains, expand, bias, shrink)


def norm_pull(back, xhat, scale, gain):
    weighted = back * gain
    mean = jnp.mean(weighted, axis=-1, keepdims=True)
    along = jnp.mean(weighted * xhat, axis=-1, keepdims=True)
    return (weighted - mean - xhat * along) * scale, jnp.sum(back * xhat, axis=0), jnp.sum(back, axis=0)


def on_device(
    layer_input,
    attn_norm_gain,
    attn_norm_bias,
    mlp_norm_gain,
    mlp_norm_bias,
    qkv_weight,
    qkv_bias,
    dense_weight,
    dense_bias,
    expand_weight,
    expand_bias,
    shrink_weight,
    shrink_bias,
    positions,
    pair_table,
    cotangent,
):
    count = lax.axis_size("ctx")
    me = lax.axis_index("ctx")
    rows = layer_input.shape[0]
    block_len = rows // 2
    heads = dense_weight.shape[0] // HD
    width = layer_input.shape[1]

    place = lax.axis_index("tp")
    me_table = me.reshape(1).astype(jnp.int32)
    share = own_share(layer_input)
    cot_share = own_share(after(cotangent, share))
    cot_all = lax.all_gather(cot_share, ("ctx", "tp"), axis=0, tiled=True)

    pairs = pair_table[0]
    blocks = jnp.stack([pairs, 2 * count - 1 - pairs], axis=1).reshape(-1)
    offsets = jnp.arange(block_len, dtype=jnp.int32)
    order = (blocks[:, None] * block_len + offsets).reshape(-1)
    own_order = lax.dynamic_slice_in_dim(order, me * rows, rows, 0)[:, None]
    places = positions.reshape(2 * count, block_len)[blocks].reshape(-1).astype(F32)
    frequency = 10000.0 ** (-jnp.arange(0, ROT, 2, dtype=F32) / ROT)
    angles = frequency[:, None] * places[None, :]
    turns = split_turns(angles)
    own_turns = lax.dynamic_slice_in_dim(turns, me * rows, rows, 1)
    gains = jnp.stack([attn_norm_gain, attn_norm_bias, mlp_norm_gain, mlp_norm_bias]).astype(F32)
    cols = qkv_weight.shape[1]
    spare = -cols % 128
    weight_wide = jnp.pad(qkv_weight, ((0, 0), (0, spare)))
    bias_wide = jnp.pad(qkv_bias, (0, spare)).astype(F32)[None]
    beside = (turns, own_turns, own_order, dot_nt(cotangent, dense_weight).astype(BF16))
    pieces, (turns, own_turns, own_order, back_own) = gather_pieces(share, beside)
    qkv, xhat_all = project(
        place,
        me,
        [[layer_input]] + pieces,
        gains,
        weight_wide,
        bias_wide,
        turns,
    )

    expand_bias_wide = expand_bias.astype(F32)[None]
    adq, stats = attend_queries(me_table, qkv, back_own, own_order, order[None, :], own_turns, heads)

    attended = adq[:, : heads * HD]
    input_wide = layer_input.astype(F32)
    average = jnp.mean(input_wide, axis=-1, keepdims=True)
    centered = input_wide - average
    scale = lax.rsqrt(jnp.mean(centered * centered, axis=-1, keepdims=True) + 1e-05)
    xhat = centered * scale
    got = swap(stats, "ctx", 1)
    back_all = dot_nt(after(cot_all, stats), dense_weight).astype(BF16)
    got, back_all, attended = tie(got, back_all, attended)
    pair = jnp.stack([stats, got])
    others = [swap(pair, "ctx", k) for k in range(2, count, 2)]
    partial = dot_nn(attended, dense_weight)
    others, partial, xhat = tie(others, partial, xhat)
    stats_all = jnp.concatenate([pair] + others, axis=0)

    attended, stats_all = tie(attended, stats_all)
    pieces = {k: swap(attended, "ctx", k) for k in [1] + list(range(2, count, 2))}
    qkv_grad = attend_keys(
        me_table, qkv, back_all, stats_all, own_order, order[None, :], own_turns, adq, heads
    )
    qkv_grad_all = lax.all_gather(qkv_grad, "ctx", axis=0, tiled=True)
    pieces, qkv_grad, xhat_all = tie(pieces, qkv_grad, xhat_all)
    far = {k: swap(pieces[k - 1], "ctx", 1) for k in range(3, count, 2)}
    active, hidden_grad = gelu_branch(
        xhat_all, cot_all, gains, expand_weight, expand_bias_wide, shrink_weight
    )

    far, active, hidden_grad = tie(far, active, hidden_grad)
    pieces.update(far)
    active_own = lax.dynamic_slice_in_dim(active, me * rows, rows, 0)
    hidden_grad_own = lax.dynamic_slice_in_dim(hidden_grad, me * rows, rows, 0)
    partial = partial + dot_nn(active_own, shrink_weight)
    attn_back = dot_nt(qkv_grad, qkv_weight)
    mlp_back = dot_nt(hidden_grad_own, expand_weight)
    attn_part, attn_gain_grad, attn_bias_grad = norm_pull(attn_back, xhat, scale, gains[0:1])
    mlp_part, mlp_gain_grad, mlp_bias_grad = norm_pull(mlp_back, xhat, scale, gains[2:3])
    norm_grads = jnp.stack([attn_gain_grad, attn_bias_grad, mlp_gain_grad, mlp_bias_grad])
    own_sums = column_sums(qkv_grad).reshape(-1, HD)
    both = jnp.stack([partial, attn_part + mlp_part])
    both, norm_grads, own_sums, active, hidden_grad = tie(both, norm_grads, own_sums, active, hidden_grad)

    def normed_product(xhat_all, grad, gain, bias):
        sums = column_sums(grad)
        return gain[:, None] * dot_tn(xhat_all, grad) + bias[:, None] * sums[None, :], sums

    def qkv_product(xhat_all, grad, sums):
        sums = column_sums(grad) if sums is None else sums.reshape(-1)
        return gains[0][:, None] * dot_tn(xhat_all, grad) + gains[1][:, None] * sums[None, :]

    def dense_product(cot_all):
        return dense_weight_grads(me_table, cot_all, [attended] + [pieces[k] for k in range(1, count)])

    (both, norm_grads, qkv_bias_grad), results = overlap(
        [sum_tp(both), sum_small(norm_grads, ("tp", "ctx")), sum_small(own_sums, ("ctx",))],
        [
            (dot_tn, (active, cot_all)),
            (normed_product, (xhat_all, hidden_grad, gains[2], gains[3])),
            (dense_product, (cot_all,)),
            (column_sums, (cot_all,)),
            (qkv_product, lambda ends: (xhat_all, qkv_grad_all, ends.get(2))),
        ],
    )
    shrink_grad, (expand_grad, expand_bias_grad), dense_grad, bias_grad, qkv_weight_grad = results
    qkv_bias_grad = qkv_bias_grad.reshape(-1)
    bias_total = dense_bias.astype(F32) + shrink_bias.astype(F32)
    layer_output = (input_wide + both[0].astype(F32) + bias_total).astype(BF16)
    input_grad = cotangent.astype(F32) + both[1].astype(F32)
    return (
        layer_output,
        input_grad,
        norm_grads[0],
        norm_grads[1],
        norm_grads[2],
        norm_grads[3],
        qkv_weight_grad,
        qkv_bias_grad,
        dense_grad,
        bias_grad,
        expand_grad,
        expand_bias_grad,
        shrink_grad,
        bias_grad,
    )


def solution(mesh):
    placed = (
        P("ctx", None),
        P(),
        P(),
        P(),
        P(),
        P(None, "tp"),
        P("tp"),
        P("tp", None),
        P(),
        P(None, "tp"),
        P("tp"),
        P("tp", None),
        P(),
        P(),
        P(),
        P("ctx", None),
    )
    return jax.shard_map(
        on_device,
        mesh=mesh,
        in_specs=placed,
        out_specs=(
            P("ctx", None),
            P("ctx", None),
            P(),
            P(),
            P(),
            P(),
            P(None, "tp"),
            P("tp"),
            P("tp", None),
            P(),
            P(None, "tp"),
            P("tp"),
            P("tp", None),
            P(),
        ),
        check_vma=False,
    )
```
